128 devices in a mesh: dp: 16 (over x, z), mp: 8 (over y, core).
Axes of the slice: x: 4, y: 4, z: 4, core: 2. Of those that a mesh axis runs over, the one named last changes fastest.
Arguments:
- query: bfloat16 [4, 1280, 8192], P(None, 'dp', 'mp'), may hold values from -80 to 80
- token_keys: bfloat16 [4, 1280, 1024], P(None, 'dp', 'mp'), may hold values from -5 to 5
- token_values: bfloat16 [4, 1280, 1024], P(None, 'dp', 'mp'), may hold values from -5 to 5
- cache_keys: bfloat16 [1280, 8, 128, 128], P('dp', 'mp'), may hold values from -4 to 4
- stored_values: bfloat16 [1280, 8, 128, 128], P('dp', 'mp'), may hold values from -5 to 5
- lengths: int32 [1280], P('dp'), may hold values from 1 to 128, as said below
- talker_row: int32 [1280], P('dp'), may hold values from 0 to 1279, as said below
- residual: bfloat16 [4, 1280, 8192], P(None, 'dp', 'mp'), may hold values from -2 to 2
- embedding: bfloat16 [4, 1280, 8192], P(None, 'dp', 'mp'), may hold values from -6 to 6
- out_weight: bfloat16 [8192, 8192], P('mp'), may hold values from -0.0625 to 0.0625
- talker_proj: bfloat16 [8192, 3584], P(None, 'mp'), may hold values from -2 to 2
- talker_gain: bfloat16 [3584], P('mp'), may hold values from 0.25 to 1.75
Outputs:
- hidden: bfloat16 [4, 1280, 8192], P(None, 'dp', 'mp')
- talker_input: bfloat16 [4, 1280, 3584], P(None, 'dp', 'mp')
The draws below stay inside these ranges and needn't reach their ends.
Inputs may be any that keep to these rules, and one draw needn't show every extreme that they name: `lengths`: some stream has all 128 slots filled. `talker_row`: A permutation of the streams. Streams of one index of dp (rows of one device) land in at most 10 rows of any one talker shard of 80 rows, and exactly 10 in every shard they reach.
All inputs are finite; a program needn't handle non-finite values.
Results may differ from the reference program's by a relative error of at most 0.015.
Values may be sent and summed in bfloat16 or wider, within the bound.
No kernel may reach another device: no remote copies, remote signals or barrier semaphores. Data moves between devices by JAX's collectives and lax.ppermute only.
A program may use at most 128 MiB of HBM per device.

```python
import jax
import jax.numpy as jnp
from jax import lax

D = 8192
DT = 3584
QUERY_HEADS = 64
KEY_VALUE_HEADS = 8
HEAD_SIZE = 128
CACHE_SLOTS = 128
S_DEV = 80
DECODE_STEPS = 4
STREAM_TOTAL = 1280
CAP = 10
N_DP = 16
N_MP = 8


def shared_keys(key):
    return jnp.clip(jax.random.normal(key, (STREAM_TOTAL, KEY_VALUE_HEADS, CACHE_SLOTS, HEAD_SIZE), jnp.float32), -4.0, 4.0)


def draw_cache_keys(key, part):
    starting_keys = shared_keys(key)
    return starting_keys.astype(jnp.bfloat16)


def draw_query(key, part):
    key = jax.random.fold_in(key, 12)
    fresh = jnp.clip(jax.random.normal(key, (DECODE_STEPS, STREAM_TOTAL, QUERY_HEADS * HEAD_SIZE), jnp.float32), -6.0, 6.0)
    return fresh.astype(jnp.bfloat16)


def draw_lengths(key, part):
    key = jax.random.fold_in(key, 14)
    first_key, second_key = jax.random.split(key)
    boost = jax.random.randint(first_key, (N_DP, 1), 1, 5)
    base_len = jax.random.randint(second_key, (N_DP, S_DEV), 0, CACHE_SLOTS)
    filled = jnp.minimum(CACHE_SLOTS, 1 + base_len * boost // 4)
    filled = filled.at[0, 0].set(CACHE_SLOTS)
    return filled.reshape(STREAM_TOTAL).astype(jnp.int32)


def draw_talker_row(key, part):
    key = jax.random.fold_in(key, 13)
    first_key, second_key, third_key = jax.random.split(key, 3)
    labels = jax.random.permutation(first_key, N_DP)
    source = jnp.arange(STREAM_TOTAL) // S_DEV
    within = jnp.arange(STREAM_TOTAL) % S_DEV
    shuffled = jax.vmap(lambda each: jax.random.permutation(each, S_DEV))(jax.random.split(second_key, N_DP))
    slot_order = shuffled[source, within]
    label_here = labels[source]
    target = (label_here + 2 * (slot_order // CAP)) % N_DP
    position = label_here // 2 * CAP + slot_order % CAP
    mixing = jax.vmap(lambda each: jax.random.permutation(each, S_DEV))(jax.random.split(third_key, N_DP))
    return (target * S_DEV + mixing[target, position]).astype(jnp.int32)


def draw_talker_proj(key, part):
    key = jax.random.fold_in(key, 15)
    first_key, second_key = jax.random.split(key)
    columns = jnp.arange(DT).astype(jnp.float32)
    column_scale = 10.0 ** jax.random.uniform(second_key, (DT,), jnp.float32) * 3.0 ** (columns / DT)
    entries = jax.random.normal(first_key, (D, DT), jnp.float32)
    return jnp.clip(entries * column_scale / (3.0 * D ** 0.5), -2.0, 2.0).astype(jnp.bfloat16)


def steps_of(key, dims, shards, smallest, high):
    loudness = 1.0
    for dim, parts in shards:
        draws = jax.random.uniform(jax.random.fold_in(jax.random.fold_in(key, 6), dim), (parts,), jnp.float32, smallest / len(shards), high / len(shards))
        loudness = loudness * jnp.repeat(jnp.exp(draws), dims[dim] // parts).reshape((-1,) + (1,) * (len(dims) - 1 - dim))
    return loudness


def bell_draw(rng, extent, spread, reach, cuts=(), kind=jnp.bfloat16):
    values = spread * jax.random.normal(rng, extent, jnp.float32)
    if cuts:
        values = values * steps_of(rng, extent, cuts, -0.22, 0.18)
    return jnp.clip(values, -reach, reach).astype(kind)


def setup_inputs(seed: int = 0) -> dict:
    key_list = jax.random.split(jax.random.key(seed), 13)
    return {
        "query": draw_query(jax.random.fold_in(key_list[12], 71), 0),
        "token_keys": bell_draw(key_list[1], (DECODE_STEPS, STREAM_TOTAL, KEY_VALUE_HEADS * HEAD_SIZE), 1.0, 5.0, ((1, 16), (2, 8))),
        "token_values": bell_draw(key_list[2], (DECODE_STEPS, STREAM_TOTAL, KEY_VALUE_HEADS * HEAD_SIZE), 1.0, 5.0, ((1, 16), (2, 8))),
        "cache_keys": draw_cache_keys(jax.random.fold_in(key_list[12], 71), 0),
        "stored_values": bell_draw(key_list[4], (STREAM_TOTAL, KEY_VALUE_HEADS, CACHE_SLOTS, HEAD_SIZE), 1.0, 5.0, ((0, 16), (1, 8))),
        "lengths": draw_lengths(jax.random.fold_in(key_list[12], 71), 0),
        "talker_row": draw_talker_row(jax.random.fold_in(key_list[12], 71), 0),
        "residual": bell_draw(key_list[7], (DECODE_STEPS, STREAM_TOTAL, D), 0.3, 2.0, ((1, 16), (2, 8))),
        "embedding": bell_draw(key_list[8], (DECODE_STEPS, STREAM_TOTAL, D), 1.0, 6.0, ((1, 16), (2, 8))),
        "out_weight": bell_draw(key_list[9], (QUERY_HEADS * HEAD_SIZE, D), (QUERY_HEADS * HEAD_SIZE) ** -0.5, 0.0625, ((0, 8),)),
        "talker_proj": draw_talker_proj(jax.random.fold_in(key_list[12], 71), 0),
        "talker_gain": jnp.clip(1.0 + 0.15 * jax.random.normal(key_list[11], (DT,), jnp.float32), 0.25, 1.75).astype(jnp.bfloat16),
    }


def reference(query, token_keys, token_values, cache_keys, stored_values, lengths, talker_row, residual, embedding, out_weight, talker_proj, talker_gain):
    query_groups = QUERY_HEADS // KEY_VALUE_HEADS
    score_scale = 1.0 / HEAD_SIZE ** 0.5
    query_rows = query.astype(jnp.float32).reshape(DECODE_STEPS, STREAM_TOTAL, KEY_VALUE_HEADS, query_groups, HEAD_SIZE)
    cache_scores = jnp.einsum('tbkgd,bkld->tbkgl', query_rows, cache_keys.astype(jnp.float32)) * score_scale
    filled = jnp.arange(CACHE_SLOTS, dtype=jnp.int32)[None, :] < lengths[:, None]
    cache_scores = jnp.where(filled[None, :, None, None, :], cache_scores, jnp.float32(-1e+30))
    recent_keys = token_keys.astype(jnp.float32).reshape(DECODE_STEPS, STREAM_TOTAL, KEY_VALUE_HEADS, HEAD_SIZE)
    fresh_scores = jnp.einsum('tbkgd,ubkd->tbkgu', query_rows, recent_keys) * score_scale
    causal = jnp.arange(DECODE_STEPS)[None, :] <= jnp.arange(DECODE_STEPS)[:, None]
    fresh_scores = jnp.where(causal[:, None, None, None, :], fresh_scores, jnp.float32(-1e+30))
    highest = jnp.maximum(lax.optimization_barrier(jnp.max(cache_scores, -1)), lax.optimization_barrier(jnp.max(fresh_scores, -1)))[..., None]
    cache_exp = jnp.exp(cache_scores - highest)
    fresh_exp = jnp.exp(fresh_scores - highest)
    denominator = lax.optimization_barrier(jnp.sum(cache_exp, -1, keepdims=True)) + lax.optimization_barrier(jnp.sum(fresh_exp, -1, keepdims=True))
    cache_weights = (cache_exp / denominator).astype(jnp.bfloat16)
    fresh_weights = (fresh_exp / denominator).astype(jnp.bfloat16)
    recent_values = token_values.astype(jnp.float32).reshape(DECODE_STEPS, STREAM_TOTAL, KEY_VALUE_HEADS, HEAD_SIZE)
    context = jnp.einsum('tbkgl,bkld->tbkgd', cache_weights.astype(jnp.float32), stored_values.astype(jnp.float32))
    context = context + jnp.einsum('tbkgu,ubkd->tbkgd', fresh_weights.astype(jnp.float32), recent_values)
    context = context.astype(jnp.bfloat16).reshape(DECODE_STEPS * STREAM_TOTAL, QUERY_HEADS * HEAD_SIZE)
    block_cols = QUERY_HEADS * HEAD_SIZE // N_MP
    projected = jnp.zeros((DECODE_STEPS * STREAM_TOTAL, D), jnp.float32)
    for block in range(N_MP):
        part_ctx = context[:, block * block_cols:(block + 1) * block_cols]
        part_w = out_weight[block * block_cols:(block + 1) * block_cols]
        head_part = jnp.dot(part_ctx, part_w, preferred_element_type=jnp.float32).astype(jnp.bfloat16)
        projected = projected + head_part.astype(jnp.float32)
    projected = projected.reshape(DECODE_STEPS, STREAM_TOTAL, D)
    hidden = (residual.astype(jnp.float32) + projected).astype(jnp.bfloat16)
    mixed = jnp.dot(hidden.reshape(DECODE_STEPS * STREAM_TOTAL, D), talker_proj, preferred_element_type=jnp.float32)
    mixed = mixed + jnp.dot(embedding.reshape(DECODE_STEPS * STREAM_TOTAL, D), talker_proj, preferred_element_type=jnp.float32)
    mixed = mixed.reshape(DECODE_STEPS, STREAM_TOTAL, DT)
    meansq = lax.optimization_barrier(jnp.mean(mixed * mixed, -1, keepdims=True))
    normed = (mixed * jax.lax.rsqrt(meansq + 1e-06) * talker_gain.astype(jnp.float32)).astype(jnp.bfloat16)
    placed = jnp.zeros((DECODE_STEPS, STREAM_TOTAL, DT), jnp.bfloat16).at[:, talker_row].set(normed)
    return (hidden, placed)
```

```python
import jax
import jax.numpy as jnp
from jax import lax
from jax.sharding import PartitionSpec as P

epsilon = 1e-06
CAP = 10


def attend(query, token_keys, token_values, cache_keys, stored_values, lengths):
    step_count, row_count, query_cols = query.shape
    head_dim = cache_keys.shape[3]
    kv_local = cache_keys.shape[1]
    slot_count = cache_keys.shape[2]
    query_groups = query_cols // (kv_local * head_dim)
    score_scale = 1.0 / head_dim**0.5
    query_rows = query.reshape(step_count, row_count, kv_local, query_groups, head_dim)
    cache_scores = (
        jnp.einsum("tskgd,skld->tskgl", query_rows, cache_keys, preferred_element_type=jnp.float32)
        * score_scale
    )
    filled = jnp.arange(slot_count, dtype=jnp.int32)[None, :] < lengths[:, None]
    cache_scores = jnp.where(filled[None, :, None, None, :], cache_scores, jnp.float32(-1e30))
    recent_keys = token_keys.reshape(step_count, row_count, kv_local, head_dim)
    fresh_scores = (
        jnp.einsum("tskgd,uskd->tskgu", query_rows, recent_keys, preferred_element_type=jnp.float32)
        * score_scale
    )
    causal = jnp.arange(step_count)[None, :] <= jnp.arange(step_count)[:, None]
    fresh_scores = jnp.where(causal[:, None, None, None, :], fresh_scores, jnp.float32(-1e30))
    highest = jnp.maximum(jnp.max(cache_scores, -1), jnp.max(fresh_scores, -1))[..., None]
    cache_exp = jnp.exp(cache_scores - highest)
    fresh_exp = jnp.exp(fresh_scores - highest)
    denominator = jnp.sum(cache_exp, -1, keepdims=True) + jnp.sum(fresh_exp, -1, keepdims=True)
    cache_weights = (cache_exp / denominator).astype(jnp.bfloat16)
    fresh_weights = (fresh_exp / denominator).astype(jnp.bfloat16)
    recent_values = token_values.reshape(step_count, row_count, kv_local, head_dim)
    context = jnp.einsum(
        "tskgl,skld->tskgd", cache_weights, stored_values, preferred_element_type=jnp.float32
    )
    context = context + jnp.einsum(
        "tskgu,uskd->tskgd", fresh_weights, recent_values, preferred_element_type=jnp.float32
    )
    return context.astype(jnp.bfloat16).reshape(step_count * row_count, query_cols)


def local(
    query,
    token_keys,
    token_values,
    cache_keys,
    stored_values,
    lengths,
    talker_row,
    residual,
    embedding,
    out_weight,
    talker_proj,
    talker_gain,
):
    step_count, row_count, query_cols = query.shape
    n_dp = lax.axis_size("dp")
    shard = talker_row // row_count
    place = talker_row % row_count
    same = shard[None, :] == shard[:, None]
    earlier = jnp.arange(row_count)[None, :] < jnp.arange(row_count)[:, None]
    slot = shard * CAP + jnp.sum((same & earlier).astype(jnp.int32), 1)
    pick = slot[None, :] == jnp.arange(n_dp * CAP, dtype=jnp.int32)[:, None]
    sent_place = jnp.sum(jnp.where(pick, place[None, :] + 1, 0), 1).reshape(n_dp, CAP) - 1
    got_place = lax.all_to_all(sent_place, "dp", 0, 0, tiled=True).reshape(n_dp * CAP)

    context = attend(query, token_keys, token_values, cache_keys, stored_values, lengths)
    head_partial = jnp.dot(context, out_weight, preferred_element_type=jnp.float32).reshape(
        step_count, row_count, -1
    )
    summed = lax.psum_scatter(
        head_partial.astype(jnp.bfloat16), "mp", scatter_dimension=2, tiled=True
    ).astype(jnp.float32)
    hidden = (residual.astype(jnp.float32) + summed).astype(jnp.bfloat16)
    both = hidden + embedding
    piece = lax.all_gather(both, "mp", axis=2, tiled=True)
    mixed = jnp.einsum("tsd,dc->tsc", piece, talker_proj, preferred_element_type=jnp.float32)
    talk_cols = talker_proj.shape[1]
    squares = lax.psum(jnp.sum(mixed * mixed, -1), "mp")
    talk_width = talk_cols * lax.axis_size("mp")
    normed = (
        mixed
        * lax.rsqrt(squares / talk_width + epsilon)[..., None]
        * talker_gain.astype(jnp.float32)
    ).astype(jnp.bfloat16)
    sent = jnp.einsum("ks,tsc->ktc", pick.astype(jnp.bfloat16), normed)
    got = lax.all_to_all(sent, "dp", 0, 0, tiled=True)
    put = got_place[None, :] == jnp.arange(row_count, dtype=jnp.int32)[:, None]
    talker_input = jnp.einsum("sk,ktc->tsc", put.astype(jnp.bfloat16), got)
    return (hidden, talker_input.astype(jnp.bfloat16))


def solution(mesh):
    placed = (
        P(None, "dp", "mp"),
        P(None, "dp", "mp"),
        P(None, "dp", "mp"),
        P("dp", "mp", None, None),
        P("dp", "mp", None, None),
        P("dp"),
        P("dp"),
        P(None, "dp", "mp"),
        P(None, "dp", "mp"),
        P("mp", None),
        P(None, "mp"),
        P("mp"),
    )
    return jax.shard_map(
        local,
        mesh=mesh,
        in_specs=placed,
        out_specs=(P(None, "dp", "mp"), P(None, "dp", "mp")),
        check_vma=False,
    )
```

```python
import jax
import jax.numpy as jnp
from jax import lax
from jax.experimental import pallas as pl
from jax.experimental.pallas import tpu as pltpu
from jax.sharding import PartitionSpec as P

epsilon = 1e-06
CAP = 10


def attend_and_project(query, token_keys, token_values, cache_keys, stored_values, lengths, out_weight, blocks):
    step_count, row_count, query_cols = query.shape
    head_dim = cache_keys.shape[-1]
    slot_count = cache_keys.shape[-2]
    groups = query_cols // head_dim
    streams = 16
    each = step_count * groups
    fresh = step_count * streams
    padded = max(fresh, slot_count)
    chunks = row_count // streams
    rows = step_count * row_count
    count = blocks.shape[0]
    cols = query_cols
    scale = 1.0 / head_dim**0.5

    def body(blocks_ref, len_ref, q_ref, tk_ref, tv_ref, k_ref, v_ref, w_ref, ctx_ref, *rest):
        out_refs, (w_buf, sems) = rest[:count], rest[count:]
        chunk = pl.program_id(0)

        def load(k):
            at = pl.ds(pl.multiple_of(blocks_ref[k] * cols, cols), cols)
            return pltpu.make_async_copy(w_ref.at[:, at], w_buf.at[k], sems.at[k])

        @pl.when(chunk == 0)
        def _():
            for k in range(count):
                load(k).start()

        q = q_ref[...].reshape(step_count, streams, groups, head_dim)
        q = jnp.swapaxes(q, 0, 1).reshape(streams, each, head_dim)
        scores = (
            lax.dot_general(
                q, k_ref[...], (((2,), (2,)), ((0,), (0,))), preferred_element_type=jnp.float32
            )
            * scale
        )
        slot = lax.broadcasted_iota(jnp.int32, (1, 1, slot_count), 2)
        filled = jnp.concatenate(
            [slot < len_ref[chunk * streams + b] for b in range(streams)]
        )
        scores = jnp.where(filled, scores, -1e30)
        q = q.reshape(streams * each, head_dim)
        copies = padded // fresh
        keys = jnp.concatenate([tk_ref[...].reshape(fresh, head_dim)] * copies)
        values = jnp.concatenate([tv_ref[...].reshape(fresh, head_dim)] * copies)
        recent = (
            lax.dot_general(
                q,
                keys,
                (((1,), (1,)), ((), ())),
                preferred_element_type=jnp.float32,
            )
            * scale
        )
        row = lax.broadcasted_iota(jnp.int32, (streams * each, padded), 0)
        col = lax.broadcasted_iota(jnp.int32, (streams * each, padded), 1)
        mine = (row // each == col % streams) & (col // streams <= row // groups % step_count)
        recent = jnp.where(mine, recent, -1e30).reshape(streams, each, padded)
        highest = jnp.max(jnp.maximum(scores, recent), -1, keepdims=True)
        scores, recent = jnp.exp(scores - highest), jnp.exp(recent - highest)
        total = jnp.sum(scores + recent, -1, keepdims=True)
        share = 1.0 / total
        weights = (scores * share).astype(jnp.bfloat16)
        recent = (recent * share).astype(jnp.bfloat16).reshape(streams * each, padded)
        context = lax.dot_general(
            weights, v_ref[...], (((2,), (1,)), ((0,), (0,))), preferred_element_type=jnp.float32
        ).reshape(streams * each, head_dim)
        context += jnp.dot(
            recent, values, preferred_element_type=jnp.float32
        )
        context = jnp.swapaxes(context.reshape(streams, step_count, groups, head_dim), 0, 1)
        context = context.reshape(step_count, streams, cols).astype(jnp.bfloat16)
        for t in range(step_count):
            at = pl.ds(pl.multiple_of(t * row_count + chunk * streams, streams), streams)
            ctx_ref[at, :] = context[t]

        @pl.when(chunk == chunks - 1)
        def _():
            for k in range(count):
                load(k).wait()
                out_refs[k][...] = jnp.dot(
                    ctx_ref[...], w_buf[k], preferred_element_type=jnp.float32
                ).astype(jnp.bfloat16)

    def by_stream(*shape):
        return pl.BlockSpec(shape, lambda i, *_: (i,) + (0,) * (len(shape) - 1))

    def by_step(width):
        return pl.BlockSpec((step_count, streams, width), lambda i, *_: (0, i, 0))

    whole = pl.BlockSpec((rows, cols), lambda i, *_: (0, 0))
    return pl.pallas_call(
        body,
        grid_spec=pltpu.PrefetchScalarGridSpec(
            num_scalar_prefetch=2,
            grid=(chunks,),
            in_specs=[
                by_step(query_cols),
                by_step(head_dim),
                by_step(head_dim),
                by_stream(streams, slot_count, head_dim),
                by_stream(streams, slot_count, head_dim),
                pl.BlockSpec(memory_space=pltpu.HBM),
            ],
            out_specs=[whole] * (1 + count),
            scratch_shapes=[
                pltpu.VMEM((count, out_weight.shape[0], cols), jnp.bfloat16),
                pltpu.SemaphoreType.DMA((count,)),
            ],
        ),
        out_shape=[jax.ShapeDtypeStruct((rows, cols), jnp.bfloat16)] * (1 + count),
        compiler_params=pltpu.CompilerParams(vmem_limit_bytes=60 << 20),
        cost_estimate=pl.CostEstimate(
            flops=2 * count * rows * cols * cols,
            bytes_accessed=32 << 20,
            transcendentals=0,
        ),
    )(
        blocks,
        lengths,
        query,
        token_keys,
        token_values,
        cache_keys.reshape(row_count, slot_count, head_dim),
        stored_values.reshape(row_count, slot_count, head_dim),
        out_weight,
    )


def head_product(context, out_weight, blocks):
    rows, depth = context.shape
    count = blocks.shape[0]
    cols = out_weight.shape[1] // lax.axis_size("mp")

    def body(blocks_ref, context_ref, w_ref, *rest):
        out_refs, (w_buf, sems) = rest[:count], rest[count:]
        loads = []
        for k in range(count):
            at = pl.ds(pl.multiple_of(blocks_ref[k] * cols, cols), cols)
            loads.append(pltpu.make_async_copy(w_ref.at[:, at], w_buf.at[k], sems.at[k]))
            loads[k].start()
        for k in range(count):
            loads[k].wait()
            out_refs[k][...] = jnp.dot(
                context_ref[...], w_buf[k], preferred_element_type=jnp.float32
            ).astype(jnp.bfloat16)

    return pl.pallas_call(
        body,
        in_specs=[
            pl.BlockSpec(memory_space=pltpu.SMEM),
            pl.BlockSpec(memory_space=pltpu.VMEM),
            pl.BlockSpec(memory_space=pltpu.HBM),
        ],
        out_specs=[pl.BlockSpec(memory_space=pltpu.VMEM)] * count,
        out_shape=[jax.ShapeDtypeStruct((rows, cols), jnp.bfloat16)] * count,
        scratch_shapes=[
            pltpu.VMEM((count, depth, cols), jnp.bfloat16),
            pltpu.SemaphoreType.DMA((count,)),
        ],
        compiler_params=pltpu.CompilerParams(vmem_limit_bytes=50 << 20),
        cost_estimate=pl.CostEstimate(
            flops=2 * count * rows * depth * cols,
            bytes_accessed=2 * count * (depth + rows) * cols,
            transcendentals=0,
        ),
    )(blocks, context, out_weight)


def talker_product(total, pieces, proj_columns, blocks):
    depth = pieces[0][0].shape[1]
    rows = sum(part.shape[0] for part in pieces[0])
    sizes = [len(piece) for piece in pieces]
    count = len(pieces)
    cols = proj_columns.shape[0]
    first = [] if total is None else [total]
    parts = [part for piece in pieces for part in piece]

    def body(blocks_ref, w_ref, *refs):
        part_refs, refs = list(refs[: len(parts)]), refs[len(parts) :]
        out_ref, w_buf, sems = refs[len(first) :]
        loads = []
        for k in range(count):
            at = pl.ds(pl.multiple_of(blocks_ref[k] * depth, depth), depth)
            loads.append(pltpu.make_async_copy(w_ref.at[:, at], w_buf.at[k], sems.at[k]))
            loads[k].start()
        for k in range(count):
            piece = jnp.concatenate([part_refs.pop(0)[...] for _ in range(sizes[k])])
            loads[k].wait()
            product = lax.dot_general(
                piece,
                w_buf[k],
                (((1,), (1,)), ((), ())),
                preferred_element_type=jnp.float32,
            )
            if k > 0:
                out_ref[...] += product
            elif total is None:
                out_ref[...] = product
            else:
                out_ref[...] = refs[0][...] + product

    vmem = pl.BlockSpec(memory_space=pltpu.VMEM)
    return pl.pallas_call(
        body,
        in_specs=[
            pl.BlockSpec(memory_space=pltpu.SMEM),
            pl.BlockSpec(memory_space=pltpu.HBM),
        ]
        + [vmem] * len(parts + first),
        out_specs=vmem,
        out_shape=jax.ShapeDtypeStruct((rows, cols), jnp.float32),
        scratch_shapes=[
            pltpu.VMEM((count, cols, depth), jnp.bfloat16),
            pltpu.SemaphoreType.DMA((count,)),
        ],
        compiler_params=pltpu.CompilerParams(vmem_limit_bytes=20 << 20),
        cost_estimate=pl.CostEstimate(
            flops=2 * count * rows * depth * cols,
            bytes_accessed=2 * count * (depth * cols + rows * depth),
            transcendentals=0,
        ),
    )(blocks, proj_columns, *parts, *first)


def shift_y(x, by):
    count = lax.axis_size("mp")
    return lax.ppermute(x, "mp", [(i, (i + 2 * by) % count) for i in range(count)])


def swap(x):
    return lax.ppermute(x, "mp", [(i, i ^ 1) for i in range(lax.axis_size("mp"))])


def after(x, y):
    return lax.optimization_barrier((x, y))[0]


def wide(x):
    return x.astype(jnp.float32)


def narrow(x):
    return x.astype(jnp.bfloat16)


def local(
    query,
    token_keys,
    token_values,
    cache_keys,
    stored_values,
    lengths,
    talker_row,
    residual,
    embedding,
    out_weight,
    talker_proj,
    talker_gain,
):
    step_count, row_count, query_cols = query.shape
    rows = step_count * row_count
    half = rows // 2
    top, low = slice(0, half), slice(half, rows)
    n_dp = lax.axis_size("dp")
    n_mp = lax.axis_size("mp")
    mp = lax.axis_index("mp")
    y, core = mp // 2, mp % 2
    talk_cols = talker_proj.shape[1]

    def blocks(shifts):
        ids = []
        for by in shifts:
            at = (2 * y + 2 * by) % n_mp
            ids += [at + 1 - core, at + core]
        return jnp.stack(ids).astype(jnp.int32)

    context, far_away, far_here, up_away, up_here = attend_and_project(
        query, token_keys, token_values, cache_keys, stored_values, lengths, out_weight, blocks([2, 1])
    )
    far_got, up_got = swap(far_away), swap(up_away)
    down_away, down_here = head_product(context, out_weight, blocks([-1]))
    far_got, context = lax.optimization_barrier((far_got, after(context, down_here)))
    down_got = swap(down_away)
    up_far = shift_y(narrow(wide(far_here[top]) + wide(far_got[top])), 1)
    down_far = shift_y(narrow(wide(far_here[low]) + wide(far_got[low])), -1)
    below_low = shift_y(narrow(wide(up_here[low]) + wide(up_got[low])), 1)
    down_got, context = lax.optimization_barrier((down_got, context))
    above_top = shift_y(narrow(wide(down_here[top]) + wide(down_got[top])), -1)
    own_away, own_here = head_product(context, out_weight, blocks([0]))
    own_got = swap(own_away)
    below_top = shift_y(narrow(wide(up_here[top]) + wide(up_got[top]) + wide(up_far)), 1)
    above_low = shift_y(narrow(wide(down_here[low]) + wide(down_got[low]) + wide(down_far)), -1)
    residual = residual.reshape(rows, -1)
    embedding = embedding.reshape(rows, -1)

    def finish(part, below, above):
        base = wide(residual[part]) + wide(own_here[part]) + wide(own_got[part])
        return narrow(base + wide(below) + wide(above))

    hidden_top = finish(top, below_top, above_top)
    hidden_low = finish(low, below_low, above_low)
    both_top = hidden_top + embedding[top]
    both_low = hidden_low + embedding[low]

    proj_columns = talker_proj.T
    own = [both_top, both_low]
    own_got = [swap(both_top), swap(both_low)]
    below_top, above_low = shift_y(both_top, 1), shift_y(both_low, -1)
    mixed = talker_product(None, [own_got, own], proj_columns, blocks([0]))
    both_top, both_low, mixed = lax.optimization_barrier((both_top, both_low, mixed))
    below_low, above_top = shift_y(both_low, 1), shift_y(both_top, -1)
    beyond_top, beyond_low = shift_y(below_top, 1), shift_y(above_low, -1)
    below, above = [below_top, below_low], [above_top, above_low]
    below_got = [swap(below_top), swap(below_low)]
    above_got = [swap(above_top), swap(above_low)]
    mixed = talker_product(
        mixed, [below_got, below, above_got, above], proj_columns, blocks([-1, 1])
    )
    beyond_top, beyond_low, mixed = lax.optimization_barrier((beyond_top, beyond_low, mixed))
    beyond = [beyond_top, beyond_low]
    beyond_got = [swap(beyond_top), swap(beyond_low)]
    mixed = talker_product(mixed, [beyond_got, beyond], proj_columns, blocks([2]))

    squares = jnp.sum(mixed * mixed, -1)
    squares = squares + swap(squares)
    squares = squares + shift_y(squares, 1) + shift_y(squares, -1) + shift_y(squares, 2)
    normed = (
        mixed
        * lax.rsqrt(squares / (talk_cols * n_mp) + epsilon)[:, None]
        * wide(talker_gain)
    ).astype(jnp.bfloat16)

    shard = talker_row // row_count
    place = talker_row % row_count
    same = shard[None, :] == shard[:, None]
    earlier = jnp.arange(row_count)[None, :] < jnp.arange(row_count)[:, None]
    order = jnp.sum((same & earlier).astype(jnp.int32), 1)
    step = jnp.arange(step_count, dtype=jnp.int32)[:, None]
    slot = ((shard * step_count + step) * CAP + order).reshape(rows)
    slots = n_dp * step_count * CAP
    pick = slot[None, :] == jnp.arange(slots, dtype=jnp.int32)[:, None]
    spare = -talk_cols % 128
    place_cols = jnp.broadcast_to(
        jnp.tile(narrow(place + 1), step_count)[:, None], (rows, spare)
    )
    sent = jnp.dot(narrow(pick), jnp.concatenate([normed, place_cols], 1))
    got = lax.all_to_all(
        sent.reshape(n_dp, slots // n_dp, -1), "dp", 0, 0, tiled=True
    ).reshape(slots, -1)
    got_place = got[:, talk_cols].astype(jnp.int32) - 1
    got_step = jnp.arange(slots, dtype=jnp.int32) // CAP % step_count
    got_row = jnp.where(got_place < 0, rows, got_step * row_count + got_place)
    put = got_row[None, :] == jnp.arange(rows, dtype=jnp.int32)[:, None]
    talker_input = jnp.dot(narrow(put), got[:, :talk_cols])
    hidden = jnp.concatenate([hidden_top, hidden_low])
    return (
        hidden.reshape(step_count, row_count, -1),
        talker_input.reshape(step_count, row_count, -1),
    )


def solution(mesh):
    placed = (
        P(None, "dp", "mp"),
        P(None, "dp", "mp"),
        P(None, "dp", "mp"),
        P("dp", "mp", None, None),
        P("dp", "mp", None, None),
        P("dp"),
        P("dp"),
        P(None, "dp", "mp"),
        P(None, "dp", "mp"),
        P("mp", None),
        P(None, "mp"),
        P("mp"),
    )
    return jax.shard_map(
        local,
        mesh=mesh,
        in_specs=placed,
        out_specs=(P(None, "dp", "mp"), P(None, "dp", "mp")),
        check_vma=False,
    )
```

```python
import jax
import jax.numpy as jnp
from jax import lax
from jax.experimental import pallas as pl
from jax.experimental.pallas import tpu as pltpu
from jax.sharding import PartitionSpec as P

epsilon = 1e-06
CAP = 10


def attend_and_project(query, token_keys, token_values, cache_keys, stored_values, lengths, out_weight, blocks):
    step_count, row_count, query_cols = query.shape
    head_dim = cache_keys.shape[-1]
    slot_count = cache_keys.shape[-2]
    groups = query_cols // head_dim
    streams = 16
    each = step_count * groups
    fresh = step_count * streams
    padded = max(fresh, slot_count)
    chunks = row_count // streams
    rows = step_count * row_count
    count = blocks.shape[0]
    cols = query_cols
    scale = 1.0 / head_dim**0.5

    def body(blocks_ref, len_ref, q_ref, tk_ref, tv_ref, k_ref, v_ref, w_ref, ctx_ref, *rest):
        out_refs, (w_buf, sems) = rest[:count], rest[count:]
        chunk = pl.program_id(0)

        def load(k):
            at = pl.ds(pl.multiple_of(blocks_ref[k] * cols, cols), cols)
            return pltpu.make_async_copy(w_ref.at[:, at], w_buf.at[k], sems.at[k])

        @pl.when(chunk == 0)
        def _():
            for k in range(count):
                load(k).start()

        q = q_ref[...].reshape(step_count, streams, groups, head_dim)
        q = jnp.swapaxes(q, 0, 1).reshape(streams, each, head_dim)
        scores = (
            lax.dot_general(
                q, k_ref[...], (((2,), (2,)), ((0,), (0,))), preferred_element_type=jnp.float32
            )
            * scale
        )
        slot = lax.broadcasted_iota(jnp.int32, (1, 1, slot_count), 2)
        filled = jnp.concatenate(
            [slot < len_ref[chunk * streams + b] for b in range(streams)]
        )
        scores = jnp.where(filled, scores, -1e30)
        q = q.reshape(streams * each, head_dim)
        copies = padded // fresh
        keys = jnp.concatenate([tk_ref[...].reshape(fresh, head_dim)] * copies)
        values = jnp.concatenate([tv_ref[...].reshape(fresh, head_dim)] * copies)
        recent = (
            lax.dot_general(
                q,
                keys,
                (((1,), (1,)), ((), ())),
                preferred_element_type=jnp.float32,
            )
            * scale
        )
        row = lax.broadcasted_iota(jnp.int32, (streams * each, padded), 0)
        col = lax.broadcasted_iota(jnp.int32, (streams * each, padded), 1)
        mine = (row // each == col % streams) & (col // streams <= row // groups % step_count)
        recent = jnp.where(mine, recent, -1e30).reshape(streams, each, padded)
        highest = jnp.max(jnp.maximum(scores, recent), -1, keepdims=True)
        scores, recent = jnp.exp(scores - highest), jnp.exp(recent - highest)
        total = jnp.sum(scores + recent, -1, keepdims=True)
        share = 1.0 / total
        weights = (scores * share).astype(jnp.bfloat16)
        recent = (recent * share).astype(jnp.bfloat16).reshape(streams * each, padded)
        context = lax.dot_general(
            weights, v_ref[...], (((2,), (1,)), ((0,), (0,))), preferred_element_type=jnp.float32
        ).reshape(streams * each, head_dim)
        context += jnp.dot(
            recent, values, preferred_element_type=jnp.float32
        )
        context = jnp.swapaxes(context.reshape(streams, step_count, groups, head_dim), 0, 1)
        context = context.reshape(step_count, streams, cols).astype(jnp.bfloat16)
        for t in range(step_count):
            at = pl.ds(pl.multiple_of(t * row_count + chunk * streams, streams), streams)
            ctx_ref[at, :] = context[t]

        @pl.when(chunk == chunks - 1)
        def _():
            for k in range(count):
                load(k).wait()
                out_refs[k][...] = jnp.dot(
                    ctx_ref[...], w_buf[k], preferred_element_type=jnp.float32
                ).astype(jnp.bfloat16)

    def by_stream(*shape):
        return pl.BlockSpec(shape, lambda i, *_: (i,) + (0,) * (len(shape) - 1))

    def by_step(width):
        return pl.BlockSpec((step_count, streams, width), lambda i, *_: (0, i, 0))

    whole = pl.BlockSpec((rows, cols), lambda i, *_: (0, 0))
    return pl.pallas_call(
        body,
        grid_spec=pltpu.PrefetchScalarGridSpec(
            num_scalar_prefetch=2,
            grid=(chunks,),
            in_specs=[
                by_step(query_cols),
                by_step(head_dim),
                by_step(head_dim),
                by_stream(streams, slot_count, head_dim),
                by_stream(streams, slot_count, head_dim),
                pl.BlockSpec(memory_space=pltpu.HBM),
            ],
            out_specs=[whole] * (1 + count),
            scratch_shapes=[
                pltpu.VMEM((count, out_weight.shape[0], cols), jnp.bfloat16),
                pltpu.SemaphoreType.DMA((count,)),
            ],
        ),
        out_shape=[jax.ShapeDtypeStruct((rows, cols), jnp.bfloat16)] * (1 + count),
        compiler_params=pltpu.CompilerParams(vmem_limit_bytes=40 << 20),
        cost_estimate=pl.CostEstimate(
            flops=2 * count * rows * cols * cols,
            bytes_accessed=32 << 20,
            transcendentals=0,
        ),
    )(
        blocks,
        lengths,
        in_hbm(query),
        in_hbm(token_keys),
        in_hbm(token_values),
        in_hbm(cache_keys.reshape(row_count, slot_count, head_dim)),
        in_hbm(stored_values.reshape(row_count, slot_count, head_dim)),
        in_hbm(out_weight),
    )


def head_product(context, out_weight, blocks):
    rows, depth = context.shape
    count = blocks.shape[0]
    cols = out_weight.shape[1] // lax.axis_size("mp")

    def body(blocks_ref, context_ref, w_ref, *rest):
        out_refs, (w_buf, sems) = rest[:count], rest[count:]
        loads = []
        for k in range(count):
            at = pl.ds(pl.multiple_of(blocks_ref[k] * cols, cols), cols)
            loads.append(pltpu.make_async_copy(w_ref.at[:, at], w_buf.at[k], sems.at[k]))
            loads[k].start()
        for k in range(count):
            loads[k].wait()
            out_refs[k][...] = jnp.dot(
                context_ref[...], w_buf[k], preferred_element_type=jnp.float32
            ).astype(jnp.bfloat16)

    return pl.pallas_call(
        body,
        in_specs=[
            pl.BlockSpec(memory_space=pltpu.SMEM),
            pl.BlockSpec(memory_space=pltpu.VMEM),
            pl.BlockSpec(memory_space=pltpu.HBM),
        ],
        out_specs=[pl.BlockSpec(memory_space=pltpu.VMEM)] * count,
        out_shape=[jax.ShapeDtypeStruct((rows, cols), jnp.bfloat16)] * count,
        scratch_shapes=[
            pltpu.VMEM((count, depth, cols), jnp.bfloat16),
            pltpu.SemaphoreType.DMA((count,)),
        ],
        compiler_params=pltpu.CompilerParams(vmem_limit_bytes=24 << 20),
        cost_estimate=pl.CostEstimate(
            flops=2 * count * rows * depth * cols,
            bytes_accessed=2 * count * (depth + rows) * cols,
            transcendentals=0,
        ),
    )(blocks, context, in_hbm(out_weight))


def talker_product(total, pieces, proj_columns, blocks):
    depth = pieces[0][0].shape[1]
    rows = sum(part.shape[0] for part in pieces[0])
    sizes = [len(piece) for piece in pieces]
    count = len(pieces)
    cols = proj_columns.shape[0]
    first = [] if total is None else [total]
    parts = [part for piece in pieces for part in piece]

    def body(blocks_ref, w_ref, *refs):
        part_refs, refs = list(refs[: len(parts)]), refs[len(parts) :]
        out_ref = refs[-1]
        for k in range(count):
            piece = jnp.concatenate([part_refs.pop(0)[...] for _ in range(sizes[k])])
            at = pl.ds(pl.multiple_of(blocks_ref[k] * depth, depth), depth)
            product = lax.dot_general(
                piece,
                w_ref[:, at],
                (((1,), (1,)), ((), ())),
                preferred_element_type=jnp.float32,
            )
            if k > 0:
                out_ref[...] += product
            elif total is None:
                out_ref[...] = product
            else:
                out_ref[...] = refs[0][...] + product

    vmem = pl.BlockSpec(memory_space=pltpu.VMEM)
    return pl.pallas_call(
        body,
        in_specs=[
            pl.BlockSpec(memory_space=pltpu.SMEM),
            vmem,
        ]
        + [vmem] * len(parts + first),
        out_specs=vmem,
        out_shape=jax.ShapeDtypeStruct((rows, cols), jnp.float32),
        compiler_params=pltpu.CompilerParams(vmem_limit_bytes=20 << 20),
        cost_estimate=pl.CostEstimate(
            flops=2 * count * rows * depth * cols,
            bytes_accessed=2 * count * (depth * cols + rows * depth),
            transcendentals=0,
        ),
    )(blocks, proj_columns, *parts, *first)


def shift_y(x, by):
    count = lax.axis_size("mp")
    return lax.ppermute(x, "mp", [(i, (i + 2 * by) % count) for i in range(count)])


def onward(x):
    count = lax.axis_size("mp")
    return lax.ppermute(x, "mp", [(i, (i + 2 - 4 * (i % 2)) % count) for i in range(count)])


def across(x, by):
    count = lax.axis_size("mp")
    moves = [(i, (i + 1 + 2 * by if i % 2 == 0 else i - 1 - 2 * by) % count) for i in range(count)]
    return lax.ppermute(x, "mp", moves)


def swap(x):
    return lax.ppermute(x, "mp", [(i, i ^ 1) for i in range(lax.axis_size("mp"))])


def in_hbm(x):
    return pltpu.with_memory_space_constraint(x, pltpu.HBM)


def wide(x):
    return x.astype(jnp.float32)


def narrow(x):
    return x.astype(jnp.bfloat16)


def local(
    query,
    token_keys,
    token_values,
    cache_keys,
    stored_values,
    lengths,
    talker_row,
    residual,
    embedding,
    out_weight,
    talker_proj,
    talker_gain,
):
    step_count, row_count, query_cols = query.shape
    rows = step_count * row_count
    n_dp = lax.axis_size("dp")
    n_mp = lax.axis_size("mp")
    mp = lax.axis_index("mp")
    y, core = mp // 2, mp % 2
    talk_cols = talker_proj.shape[1]

    ahead = 1 - 2 * core

    def blocks(*wanted):
        ids = [(2 * (y + shift)) % n_mp + core + other * ahead for shift, other in wanted]
        return jnp.stack(ids).astype(jnp.int32)

    context, far_away, far_here = attend_and_project(
        query,
        token_keys,
        token_values,
        cache_keys,
        stored_values,
        lengths,
        out_weight,
        blocks((2, 1), (2, 0)),
    )
    far_got = swap(far_away)
    other_away, other_here = head_product(context, out_weight, blocks((-ahead, 0), (ahead, 1)))
    far_got, other_away, context = lax.optimization_barrier((far_got, other_away, context))
    far = narrow(wide(far_here) + wide(far_got))
    far_on = onward(far)
    other_got = swap(other_away)
    other = narrow(wide(other_here) + wide(other_got))
    other, context = lax.optimization_barrier((other, context))
    other_in = across(other, 1)
    same_away, same_here, own_away, own_here = head_product(
        context, out_weight, blocks((-ahead, 1), (ahead, 0), (0, 1), (0, 0))
    )
    same_got, own_got = swap(same_away), swap(own_away)
    same_in = onward(narrow(wide(same_here) + wide(same_got) + wide(far_on)))
    residual = residual.reshape(rows, -1)
    embedding = embedding.reshape(rows, -1)

    base = wide(residual) + wide(own_here) + wide(own_got)
    hidden = narrow(base + wide(same_in) + wide(other_in))
    both = hidden + embedding

    proj_columns = talker_proj.T
    near = onward(both)
    cross = across(both, -1)
    both_got = swap(both)
    beyond = onward(near)
    mixed = talker_product(None, [[both_got], [both]], proj_columns, blocks((0, 1), (0, 0)))
    near_got = swap(near)
    mixed = talker_product(
        mixed, [[near_got], [near]], proj_columns, blocks((ahead, 1), (-ahead, 0))
    )
    cross_got = swap(cross)
    mixed = talker_product(
        mixed, [[cross_got], [cross]], proj_columns, blocks((ahead, 0), (-ahead, 1))
    )
    beyond, mixed = lax.optimization_barrier((beyond, mixed))
    mixed = talker_product(mixed, [[swap(beyond)], [beyond]], proj_columns, blocks((2, 1), (2, 0)))

    squares = jnp.sum(mixed * mixed, -1)
    squares = squares + swap(squares)
    squares = squares + shift_y(squares, 1) + shift_y(squares, -1) + shift_y(squares, 2)
    normed = (
        mixed
        * lax.rsqrt(squares / (talk_cols * n_mp) + epsilon)[:, None]
        * wide(talker_gain)
    ).astype(jnp.bfloat16)

    shard = talker_row // row_count
    place = talker_row % row_count
    same = shard[None, :] == shard[:, None]
    earlier = jnp.arange(row_count)[None, :] < jnp.arange(row_count)[:, None]
    order = jnp.sum((same & earlier).astype(jnp.int32), 1)
    step = jnp.arange(step_count, dtype=jnp.int32)[:, None]
    slot = ((shard * step_count + step) * CAP + order).reshape(rows)
    slots = n_dp * step_count * CAP
    pick = slot[None, :] == jnp.arange(slots, dtype=jnp.int32)[:, None]
    spare = -talk_cols % 128
    place_cols = jnp.broadcast_to(
        jnp.tile(narrow(place + 1), step_count)[:, None], (rows, spare)
    )
    sent = jnp.dot(narrow(pick), jnp.concatenate([normed, place_cols], 1))
    got = lax.all_to_all(
        sent.reshape(n_dp, slots // n_dp, -1), "dp", 0, 0, tiled=True
    ).reshape(slots, -1)
    got_place = got[:, talk_cols].astype(jnp.int32) - 1
    got_step = jnp.arange(slots, dtype=jnp.int32) // CAP % step_count
    got_row = jnp.where(got_place < 0, rows, got_step * row_count + got_place)
    put = got_row[None, :] == jnp.arange(rows, dtype=jnp.int32)[:, None]
    talker_input = jnp.dot(narrow(put), got[:, :talk_cols])
    return (
        hidden.reshape(step_count, row_count, -1),
        talker_input.reshape(step_count, row_count, -1),
    )


def solution(mesh):
    placed = (
        P(None, "dp", "mp"),
        P(None, "dp", "mp"),
        P(None, "dp", "mp"),
        P("dp", "mp", None, None),
        P("dp", "mp", None, None),
        P("dp"),
        P("dp"),
        P(None, "dp", "mp"),
        P(None, "dp", "mp"),
        P("mp", None),
        P(None, "mp"),
        P("mp"),
    )
    return jax.shard_map(
        local,
        mesh=mesh,
        in_specs=placed,
        out_specs=(P(None, "dp", "mp"), P(None, "dp", "mp")),
        check_vma=False,
    )
```

```python
import jax
import jax.numpy as jnp
from jax import lax
from jax.experimental import pallas as pl
from jax.experimental.pallas import tpu as pltpu
from jax.sharding import PartitionSpec as P

epsilon = 1e-06
CAP = 10


def attend_and_project(query, token_keys, token_values, cache_keys, stored_values, lengths, out_weight, blocks):
    step_count, row_count, query_cols = query.shape
    head_dim = cache_keys.shape[-1]
    slot_count = cache_keys.shape[-2]
    groups = query_cols // head_dim
    streams = 16
    each = step_count * groups
    fresh = step_count * streams
    padded = max(fresh, slot_count)
    chunks = row_count // streams
    rows = step_count * row_count
    count = blocks.shape[0]
    cols = query_cols
    scale = 1.0 / head_dim**0.5

    def body(blocks_ref, len_ref, q_ref, tk_ref, tv_ref, k_ref, v_ref, w_ref, ctx_ref, *rest):
        out_refs, (w_buf, sems) = rest[:count], rest[count:]
        chunk = pl.program_id(0)

        def load(k):
            at = pl.ds(pl.multiple_of(blocks_ref[k] * cols, cols), cols)
            return pltpu.make_async_copy(w_ref.at[:, at], w_buf.at[k], sems.at[k])

        @pl.when(chunk == 0)
        def _():
            for k in range(count):
                load(k).start()

        q = q_ref[...].reshape(step_count, streams, groups, head_dim)
        q = jnp.swapaxes(q, 0, 1).reshape(streams, each, head_dim)
        scores = (
            lax.dot_general(
                q, k_ref[...], (((2,), (2,)), ((0,), (0,))), preferred_element_type=jnp.float32
            )
            * scale
        )
        slot = lax.broadcasted_iota(jnp.int32, (1, 1, slot_count), 2)
        filled = jnp.concatenate(
            [slot < len_ref[chunk * streams + b] for b in range(streams)]
        )
        scores = jnp.where(filled, scores, -1e30)
        q = q.reshape(streams * each, head_dim)
        copies = padded // fresh
        keys = jnp.concatenate([tk_ref[...].reshape(fresh, head_dim)] * copies)
        values = jnp.concatenate([tv_ref[...].reshape(fresh, head_dim)] * copies)
        recent = (
            lax.dot_general(
                q,
                keys,
                (((1,), (1,)), ((), ())),
                preferred_element_type=jnp.float32,
            )
            * scale
        )
        row = lax.broadcasted_iota(jnp.int32, (streams * each, padded), 0)
        col = lax.broadcasted_iota(jnp.int32, (streams * each, padded), 1)
        mine = (row // each == col % streams) & (col // streams <= row // groups % step_count)
        recent = jnp.where(mine, recent, -1e30).reshape(streams, each, padded)
        highest = jnp.max(jnp.maximum(scores, recent), -1, keepdims=True)
        scores, recent = jnp.exp(scores - highest), jnp.exp(recent - highest)
        total = jnp.sum(scores + recent, -1, keepdims=True)
        share = 1.0 / total
        weights = (scores * share).astype(jnp.bfloat16)
        recent = (recent * share).astype(jnp.bfloat16).reshape(streams * each, padded)
        context = lax.dot_general(
            weights, v_ref[...], (((2,), (1,)), ((0,), (0,))), preferred_element_type=jnp.float32
        ).reshape(streams * each, head_dim)
        context += jnp.dot(
            recent, values, preferred_element_type=jnp.float32
        )
        context = jnp.swapaxes(context.reshape(streams, step_count, groups, head_dim), 0, 1)
        context = context.reshape(step_count, streams, cols).astype(jnp.bfloat16)
        for t in range(step_count):
            at = pl.ds(pl.multiple_of(t * row_count + chunk * streams, streams), streams)
            ctx_ref[at, :] = context[t]

        @pl.when(chunk == chunks - 1)
        def _():
            for k in range(count):
                load(k).wait()
                out_refs[k][...] = jnp.dot(
                    ctx_ref[...], w_buf[k], preferred_element_type=jnp.float32
                ).astype(jnp.bfloat16)

    def by_stream(*shape):
        return pl.BlockSpec(shape, lambda i, *_: (i,) + (0,) * (len(shape) - 1))

    def by_step(width):
        return pl.BlockSpec((step_count, streams, width), lambda i, *_: (0, i, 0))

    whole = pl.BlockSpec((rows, cols), lambda i, *_: (0, 0))
    return pl.pallas_call(
        body,
        grid_spec=pltpu.PrefetchScalarGridSpec(
            num_scalar_prefetch=2,
            grid=(chunks,),
            in_specs=[
                by_step(query_cols),
                by_step(head_dim),
                by_step(head_dim),
                by_stream(streams, slot_count, head_dim),
                by_stream(streams, slot_count, head_dim),
                pl.BlockSpec(memory_space=pltpu.HBM),
            ],
            out_specs=[whole] * (1 + count),
            scratch_shapes=[
                pltpu.VMEM((count, out_weight.shape[0], cols), jnp.bfloat16),
                pltpu.SemaphoreType.DMA((count,)),
            ],
        ),
        out_shape=[jax.ShapeDtypeStruct((rows, cols), jnp.bfloat16)] * (1 + count),
        compiler_params=pltpu.CompilerParams(vmem_limit_bytes=40 << 20),
        cost_estimate=pl.CostEstimate(
            flops=2 * count * rows * cols * cols,
            bytes_accessed=32 << 20,
            transcendentals=0,
        ),
    )(
        blocks,
        lengths,
        in_hbm(query),
        in_hbm(token_keys),
        in_hbm(token_values),
        in_hbm(cache_keys.reshape(row_count, slot_count, head_dim)),
        in_hbm(stored_values.reshape(row_count, slot_count, head_dim)),
        in_hbm(out_weight),
    )


def head_product(context, out_weight, blocks):
    rows, depth = context.shape
    count = blocks.shape[0]
    cols = out_weight.shape[1] // lax.axis_size("mp")

    def body(blocks_ref, context_ref, w_ref, *rest):
        out_refs, (w_buf, sems) = rest[:count], rest[count:]
        loads = []
        for k in range(count):
            at = pl.ds(pl.multiple_of(blocks_ref[k] * cols, cols), cols)
            loads.append(pltpu.make_async_copy(w_ref.at[:, at], w_buf.at[k], sems.at[k]))
            loads[k].start()
        for k in range(count):
            loads[k].wait()
            out_refs[k][...] = jnp.dot(
                context_ref[...], w_buf[k], preferred_element_type=jnp.float32
            ).astype(jnp.bfloat16)

    return pl.pallas_call(
        body,
        in_specs=[
            pl.BlockSpec(memory_space=pltpu.SMEM),
            pl.BlockSpec(memory_space=pltpu.VMEM),
            pl.BlockSpec(memory_space=pltpu.HBM),
        ],
        out_specs=[pl.BlockSpec(memory_space=pltpu.VMEM)] * count,
        out_shape=[jax.ShapeDtypeStruct((rows, cols), jnp.bfloat16)] * count,
        scratch_shapes=[
            pltpu.VMEM((count, depth, cols), jnp.bfloat16),
            pltpu.SemaphoreType.DMA((count,)),
        ],
        compiler_params=pltpu.CompilerParams(vmem_limit_bytes=28 << 20),
        cost_estimate=pl.CostEstimate(
            flops=2 * count * rows * depth * cols,
            bytes_accessed=2 * count * (depth + rows) * cols,
            transcendentals=0,
        ),
    )(blocks, context, in_hbm(out_weight))


def talker_product(total, pieces, proj_columns, blocks):
    depth = pieces[0][0].shape[1]
    rows = sum(part.shape[0] for part in pieces[0])
    sizes = [len(piece) for piece in pieces]
    count = len(pieces)
    cols = proj_columns.shape[0]
    first = [] if total is None else [total]
    parts = [part for piece in pieces for part in piece]

    def body(blocks_ref, w_ref, *refs):
        part_refs, refs = list(refs[: len(parts)]), refs[len(parts) :]
        out_ref = refs[-1]
        for k in range(count):
            piece = jnp.concatenate([part_refs.pop(0)[...] for _ in range(sizes[k])])
            at = pl.ds(pl.multiple_of(blocks_ref[k] * depth, depth), depth)
            product = lax.dot_general(
                piece,
                w_ref[:, at],
                (((1,), (1,)), ((), ())),
                preferred_element_type=jnp.float32,
            )
            if k > 0:
                out_ref[...] += product
            elif total is None:
                out_ref[...] = product
            else:
                out_ref[...] = refs[0][...] + product

    vmem = pl.BlockSpec(memory_space=pltpu.VMEM)
    return pl.pallas_call(
        body,
        in_specs=[
            pl.BlockSpec(memory_space=pltpu.SMEM),
            vmem,
        ]
        + [vmem] * len(parts + first),
        out_specs=vmem,
        out_shape=jax.ShapeDtypeStruct((rows, cols), jnp.float32),
        compiler_params=pltpu.CompilerParams(vmem_limit_bytes=20 << 20),
        cost_estimate=pl.CostEstimate(
            flops=2 * count * rows * depth * cols,
            bytes_accessed=2 * count * (depth * cols + rows * depth),
            transcendentals=0,
        ),
    )(blocks, proj_columns, *parts, *first)


def shift_y(x, by):
    count = lax.axis_size("mp")
    return lax.ppermute(x, "mp", [(i, (i + 2 * by) % count) for i in range(count)])


def onward(x):
    count = lax.axis_size("mp")
    return lax.ppermute(x, "mp", [(i, (i + 2 - 4 * (i % 2)) % count) for i in range(count)])


def across(x, by):
    count = lax.axis_size("mp")
    moves = [(i, (i + 1 + 2 * by if i % 2 == 0 else i - 1 - 2 * by) % count) for i in range(count)]
    return lax.ppermute(x, "mp", moves)


def swap(x):
    return lax.ppermute(x, "mp", [(i, i ^ 1) for i in range(lax.axis_size("mp"))])


def in_hbm(x):
    return pltpu.with_memory_space_constraint(x, pltpu.HBM)


def wide(x):
    return x.astype(jnp.float32)


def narrow(x):
    return x.astype(jnp.bfloat16)


def local(
    query,
    token_keys,
    token_values,
    cache_keys,
    stored_values,
    lengths,
    talker_row,
    residual,
    embedding,
    out_weight,
    talker_proj,
    talker_gain,
):
    step_count, row_count, query_cols = query.shape
    rows = step_count * row_count
    n_dp = lax.axis_size("dp")
    n_mp = lax.axis_size("mp")
    mp = lax.axis_index("mp")
    y, core = mp // 2, mp % 2
    talk_cols = talker_proj.shape[1]

    ahead = 1 - 2 * core

    def blocks(*wanted):
        ids = [(2 * (y + shift)) % n_mp + core + other * ahead for shift, other in wanted]
        return jnp.stack(ids).astype(jnp.int32)

    context, far_away, far_here = attend_and_project(
        query,
        token_keys,
        token_values,
        cache_keys,
        stored_values,
        lengths,
        out_weight,
        blocks((2, 1), (2, 0)),
    )
    far = narrow(wide(far_here) + wide(swap(far_away)))
    far, context = lax.optimization_barrier((far, context))
    far_on = onward(far)
    other_away, other_here, same_away, same_here, own_away, own_here = head_product(
        context,
        out_weight,
        blocks((-ahead, 0), (ahead, 1), (-ahead, 1), (ahead, 0), (0, 1), (0, 0)),
    )
    other_got, same_got = swap(other_away), swap(same_away)
    other = narrow(wide(other_here) + wide(other_got))
    far_on, own_away = lax.optimization_barrier((far_on, own_away))
    own_got = swap(own_away)
    other_in = across(other, 1)
    same_in = onward(narrow(wide(same_here) + wide(same_got) + wide(far_on)))
    residual = residual.reshape(rows, -1)
    embedding = embedding.reshape(rows, -1)

    base = wide(residual) + wide(own_here) + wide(own_got) + wide(other_in)
    base = lax.optimization_barrier(base)
    hidden = narrow(base + wide(same_in))
    both = hidden + embedding

    proj_columns = talker_proj.T
    near = onward(both)
    cross = across(both, -1)
    both_got = swap(both)
    beyond = onward(near)
    mixed = talker_product(None, [[both_got], [both]], proj_columns, blocks((0, 1), (0, 0)))
    near_got = swap(near)
    mixed = talker_product(
        mixed, [[near_got], [near]], proj_columns, blocks((ahead, 1), (-ahead, 0))
    )
    cross_got = swap(cross)
    mixed = talker_product(
        mixed, [[cross_got], [cross]], proj_columns, blocks((ahead, 0), (-ahead, 1))
    )
    beyond, mixed = lax.optimization_barrier((beyond, mixed))
    mixed = talker_product(mixed, [[swap(beyond)], [beyond]], proj_columns, blocks((2, 1), (2, 0)))

    squares = jnp.sum(mixed * mixed, -1)
    squares = squares + swap(squares)
    beside = onward(squares)
    squares = squares + shift_y(squares, 2) + (beside + swap(beside))
    normed = (
        mixed
        * lax.rsqrt(squares / (talk_cols * n_mp) + epsilon)[:, None]
        * wide(talker_gain)
    ).astype(jnp.bfloat16)

    shard = talker_row // row_count
    place = talker_row % row_count
    same = shard[None, :] == shard[:, None]
    earlier = jnp.arange(row_count)[None, :] < jnp.arange(row_count)[:, None]
    order = jnp.sum((same & earlier).astype(jnp.int32), 1)
    step = jnp.arange(step_count, dtype=jnp.int32)[:, None]
    slot = ((shard * step_count + step) * CAP + order).reshape(rows)
    slots = n_dp * step_count * CAP
    pick = slot[None, :] == jnp.arange(slots, dtype=jnp.int32)[:, None]
    spare = -talk_cols % 128
    place_cols = jnp.broadcast_to(
        jnp.tile(narrow(place + 1), step_count)[:, None], (rows, spare)
    )
    sent = jnp.dot(narrow(pick), jnp.concatenate([normed, place_cols], 1))
    got = lax.all_to_all(
        sent.reshape(n_dp, slots // n_dp, -1), "dp", 0, 0, tiled=True
    ).reshape(slots, -1)
    got_place = got[:, talk_cols].astype(jnp.int32) - 1
    got_step = jnp.arange(slots, dtype=jnp.int32) // CAP % step_count
    got_row = jnp.where(got_place < 0, rows, got_step * row_count + got_place)
    put = got_row[None, :] == jnp.arange(rows, dtype=jnp.int32)[:, None]
    talker_input = jnp.dot(narrow(put), got[:, :talk_cols])
    return (
        hidden.reshape(step_count, row_count, -1),
        talker_input.reshape(step_count, row_count, -1),
    )


def solution(mesh):
    placed = (
        P(None, "dp", "mp"),
        P(None, "dp", "mp"),
        P(None, "dp", "mp"),
        P("dp", "mp", None, None),
        P("dp", "mp", None, None),
        P("dp"),
        P("dp"),
        P(None, "dp", "mp"),
        P(None, "dp", "mp"),
        P("mp", None),
        P(None, "mp"),
        P("mp"),
    )
    return jax.shard_map(
        local,
        mesh=mesh,
        in_specs=placed,
        out_specs=(P(None, "dp", "mp"), P(None, "dp", "mp")),
        check_vma=False,
    )
```

```python
import jax
import jax.numpy as jnp
from jax import lax
from jax.experimental import pallas as pl
from jax.experimental.pallas import tpu as pltpu
from jax.sharding import PartitionSpec as P

epsilon = 1e-06
CAP = 10


def attend_and_project(query, token_keys, token_values, cache_keys, stored_values, lengths, out_weight, blocks):
    step_count, row_count, query_cols = query.shape
    head_dim = cache_keys.shape[-1]
    slot_count = cache_keys.shape[-2]
    groups = query_cols // head_dim
    streams = 16
    each = step_count * groups
    fresh = step_count * streams
    padded = max(fresh, slot_count)
    chunks = row_count // streams
    rows = step_count * row_count
    count = blocks.shape[0]
    cols = query_cols
    scale = 1.0 / head_dim**0.5

    def body(blocks_ref, len_ref, q_ref, tk_ref, tv_ref, k_ref, v_ref, w_ref, ctx_ref, *rest):
        out_refs, (w_buf, sems) = rest[:count], rest[count:]
        chunk = pl.program_id(0)

        def load(k):
            at = pl.ds(pl.multiple_of(blocks_ref[k] * cols, cols), cols)
            return pltpu.make_async_copy(w_ref.at[:, at], w_buf.at[k], sems.at[k])

        @pl.when(chunk == 0)
        def _():
            for k in range(count):
                load(k).start()

        q = q_ref[...].reshape(step_count, streams, groups, head_dim)
        q = jnp.swapaxes(q, 0, 1).reshape(streams, each, head_dim)
        scores = (
            lax.dot_general(
                q, k_ref[...], (((2,), (2,)), ((0,), (0,))), preferred_element_type=jnp.float32
            )
            * scale
        )
        slot = lax.broadcasted_iota(jnp.int32, (1, 1, slot_count), 2)
        filled = jnp.concatenate(
            [slot < len_ref[chunk * streams + b] for b in range(streams)]
        )
        scores = jnp.where(filled, scores, -1e30)
        q = q.reshape(streams * each, head_dim)
        copies = padded // fresh
        keys = jnp.concatenate([tk_ref[...].reshape(fresh, head_dim)] * copies)
        values = jnp.concatenate([tv_ref[...].reshape(fresh, head_dim)] * copies)
        recent = (
            lax.dot_general(
                q,
                keys,
                (((1,), (1,)), ((), ())),
                preferred_element_type=jnp.float32,
            )
            * scale
        )
        row = lax.broadcasted_iota(jnp.int32, (streams * each, padded), 0)
        col = lax.broadcasted_iota(jnp.int32, (streams * each, padded), 1)
        mine = (row // each == col % streams) & (col // streams <= row // groups % step_count)
        recent = jnp.where(mine, recent, -1e30).reshape(streams, each, padded)
        highest = jnp.max(jnp.maximum(scores, recent), -1, keepdims=True)
        scores, recent = jnp.exp(scores - highest), jnp.exp(recent - highest)
        total = jnp.sum(scores + recent, -1, keepdims=True)
        share = 1.0 / total
        weights = (scores * share).astype(jnp.bfloat16)
        recent = (recent * share).astype(jnp.bfloat16).reshape(streams * each, padded)
        context = lax.dot_general(
            weights, v_ref[...], (((2,), (1,)), ((0,), (0,))), preferred_element_type=jnp.float32
        ).reshape(streams * each, head_dim)
        context += jnp.dot(
            recent, values, preferred_element_type=jnp.float32
        )
        context = jnp.swapaxes(context.reshape(streams, step_count, groups, head_dim), 0, 1)
        context = context.reshape(step_count, streams, cols).astype(jnp.bfloat16)
        for t in range(step_count):
            at = pl.ds(pl.multiple_of(t * row_count + chunk * streams, streams), streams)
            ctx_ref[at, :] = context[t]

        @pl.when(chunk == chunks - 1)
        def _():
            for k in range(count):
                load(k).wait()
                out_refs[k][...] = jnp.dot(
                    ctx_ref[...], w_buf[k], preferred_element_type=jnp.float32
                ).astype(jnp.bfloat16)

    def by_stream(*shape):
        return pl.BlockSpec(shape, lambda i, *_: (i,) + (0,) * (len(shape) - 1))

    def by_step(width):
        return pl.BlockSpec((step_count, streams, width), lambda i, *_: (0, i, 0))

    whole = pl.BlockSpec((rows, cols), lambda i, *_: (0, 0))
    return pl.pallas_call(
        body,
        grid_spec=pltpu.PrefetchScalarGridSpec(
            num_scalar_prefetch=2,
            grid=(chunks,),
            in_specs=[
                by_step(query_cols),
                by_step(head_dim),
                by_step(head_dim),
                by_stream(streams, slot_count, head_dim),
                by_stream(streams, slot_count, head_dim),
                pl.BlockSpec(memory_space=pltpu.HBM),
            ],
            out_specs=[whole] * (1 + count),
            scratch_shapes=[
                pltpu.VMEM((count, out_weight.shape[0], cols), jnp.bfloat16),
                pltpu.SemaphoreType.DMA((count,)),
            ],
        ),
        out_shape=[jax.ShapeDtypeStruct((rows, cols), jnp.bfloat16)] * (1 + count),
        compiler_params=pltpu.CompilerParams(vmem_limit_bytes=40 << 20),
        cost_estimate=pl.CostEstimate(
            flops=2 * count * rows * cols * cols,
            bytes_accessed=32 << 20,
            transcendentals=0,
        ),
    )(
        blocks,
        in_hbm(lengths),
        in_hbm(query),
        in_hbm(token_keys),
        in_hbm(token_values),
        in_hbm(cache_keys.reshape(row_count, slot_count, head_dim)),
        in_hbm(stored_values.reshape(row_count, slot_count, head_dim)),
        in_hbm(out_weight),
    )


def head_product(context, out_weight, blocks):
    rows, depth = context.shape
    count = blocks.shape[0]
    cols = out_weight.shape[1] // lax.axis_size("mp")

    def body(blocks_ref, context_ref, w_ref, *rest):
        out_refs, (w_buf, sems) = rest[:count], rest[count:]
        loads = []
        for k in range(count):
            at = pl.ds(pl.multiple_of(blocks_ref[k] * cols, cols), cols)
            loads.append(pltpu.make_async_copy(w_ref.at[:, at], w_buf.at[k], sems.at[k]))
            loads[k].start()
        for k in range(count):
            loads[k].wait()
            out_refs[k][...] = jnp.dot(
                context_ref[...], w_buf[k], preferred_element_type=jnp.float32
            ).astype(jnp.bfloat16)

    return pl.pallas_call(
        body,
        in_specs=[
            pl.BlockSpec(memory_space=pltpu.SMEM),
            pl.BlockSpec(memory_space=pltpu.VMEM),
            pl.BlockSpec(memory_space=pltpu.HBM),
        ],
        out_specs=[pl.BlockSpec(memory_space=pltpu.VMEM)] * count,
        out_shape=[jax.ShapeDtypeStruct((rows, cols), jnp.bfloat16)] * count,
        scratch_shapes=[
            pltpu.VMEM((count, depth, cols), jnp.bfloat16),
            pltpu.SemaphoreType.DMA((count,)),
        ],
        compiler_params=pltpu.CompilerParams(vmem_limit_bytes=28 << 20),
        cost_estimate=pl.CostEstimate(
            flops=2 * count * rows * depth * cols,
            bytes_accessed=2 * count * (depth + rows) * cols,
            transcendentals=0,
        ),
    )(blocks, context, in_hbm(out_weight))


def talker_product(total, pieces, proj_columns, blocks):
    depth = pieces[0][0].shape[1]
    rows = sum(part.shape[0] for part in pieces[0])
    sizes = [len(piece) for piece in pieces]
    count = len(pieces)
    cols = proj_columns.shape[0]
    first = [] if total is None else [total]
    parts = [part for piece in pieces for part in piece]

    def body(blocks_ref, w_ref, *refs):
        part_refs, refs = list(refs[: len(parts)]), refs[len(parts) :]
        out_ref = refs[-1]
        for k in range(count):
            piece = jnp.concatenate([part_refs.pop(0)[...] for _ in range(sizes[k])])
            at = pl.ds(pl.multiple_of(blocks_ref[k] * depth, depth), depth)
            product = lax.dot_general(
                piece,
                w_ref[:, at],
                (((1,), (1,)), ((), ())),
                preferred_element_type=jnp.float32,
            )
            if k > 0:
                out_ref[...] += product
            elif total is None:
                out_ref[...] = product
            else:
                out_ref[...] = refs[0][...] + product

    vmem = pl.BlockSpec(memory_space=pltpu.VMEM)
    return pl.pallas_call(
        body,
        in_specs=[
            pl.BlockSpec(memory_space=pltpu.SMEM),
            vmem,
        ]
        + [vmem] * len(parts + first),
        out_specs=vmem,
        out_shape=jax.ShapeDtypeStruct((rows, cols), jnp.float32),
        compiler_params=pltpu.CompilerParams(vmem_limit_bytes=20 << 20),
        cost_estimate=pl.CostEstimate(
            flops=2 * count * rows * depth * cols,
            bytes_accessed=2 * count * (depth * cols + rows * depth),
            transcendentals=0,
        ),
    )(blocks, proj_columns, *parts, *first)


def shift_y(x, by):
    count = lax.axis_size("mp")
    return lax.ppermute(x, "mp", [(i, (i + 2 * by) % count) for i in range(count)])


def onward(x):
    count = lax.axis_size("mp")
    return lax.ppermute(x, "mp", [(i, (i + 2 - 4 * (i % 2)) % count) for i in range(count)])


def across(x, by):
    count = lax.axis_size("mp")
    moves = [(i, (i + 1 + 2 * by if i % 2 == 0 else i - 1 - 2 * by) % count) for i in range(count)]
    return lax.ppermute(x, "mp", moves)


def swap(x):
    return lax.ppermute(x, "mp", [(i, i ^ 1) for i in range(lax.axis_size("mp"))])


def in_hbm(x):
    return pltpu.with_memory_space_constraint(x, pltpu.HBM)


def wide(x):
    return x.astype(jnp.float32)


def narrow(x):
    return x.astype(jnp.bfloat16)


def local(
    query,
    token_keys,
    token_values,
    cache_keys,
    stored_values,
    lengths,
    talker_row,
    residual,
    embedding,
    out_weight,
    talker_proj,
    talker_gain,
):
    step_count, row_count, query_cols = query.shape
    rows = step_count * row_count
    n_dp = lax.axis_size("dp")
    n_mp = lax.axis_size("mp")
    mp = lax.axis_index("mp")
    y, core = mp // 2, mp % 2
    talk_cols = talker_proj.shape[1]

    ahead = 1 - 2 * core

    def blocks(*wanted):
        ids = [(2 * (y + shift)) % n_mp + core + other * ahead for shift, other in wanted]
        return jnp.stack(ids).astype(jnp.int32)

    context, far_away, far_here = attend_and_project(
        query,
        token_keys,
        token_values,
        cache_keys,
        stored_values,
        lengths,
        out_weight,
        blocks((2, 1), (2, 0)),
    )
    far = narrow(wide(far_here) + wide(swap(far_away)))
    far, context = lax.optimization_barrier((far, context))
    far_on = onward(far)
    other_away, other_here, same_away, same_here, own_away, own_here = head_product(
        context,
        out_weight,
        blocks((-ahead, 0), (ahead, 1), (-ahead, 1), (ahead, 0), (0, 1), (0, 0)),
    )
    other_got, same_got = swap(other_away), swap(same_away)
    other = narrow(wide(other_here) + wide(other_got))
    far_on, own_away = lax.optimization_barrier((far_on, own_away))
    own_got = swap(own_away)
    other_in = across(other, 1)
    same_in = onward(narrow(wide(same_here) + wide(same_got) + wide(far_on)))
    residual = residual.reshape(rows, -1)
    embedding = embedding.reshape(rows, -1)

    base = wide(residual) + wide(own_here) + wide(own_got) + wide(other_in)
    base = lax.optimization_barrier(base)
    hidden = narrow(base + wide(same_in))
    both = hidden + embedding

    proj_columns = talker_proj.T
    near = onward(both)
    cross = across(both, -1)
    both_got = swap(both)
    beyond = onward(near)
    mixed = talker_product(None, [[both_got], [both]], proj_columns, blocks((0, 1), (0, 0)))
    near_got = swap(near)
    mixed = talker_product(
        mixed, [[near_got], [near]], proj_columns, blocks((ahead, 1), (-ahead, 0))
    )
    cross_got = swap(cross)
    mixed = talker_product(
        mixed, [[cross_got], [cross]], proj_columns, blocks((ahead, 0), (-ahead, 1))
    )
    beyond, mixed = lax.optimization_barrier((beyond, mixed))
    mixed = talker_product(mixed, [[beyond]], proj_columns, blocks((2, 0)))
    mixed = talker_product(mixed, [[swap(beyond)]], proj_columns, blocks((2, 1)))

    squares = jnp.sum(mixed * mixed, -1)
    squares = squares + swap(squares)
    beside = onward(squares)
    squares = squares + shift_y(squares, 2) + (beside + swap(beside))
    normed = (
        mixed
        * lax.rsqrt(squares / (talk_cols * n_mp) + epsilon)[:, None]
        * wide(talker_gain)
    ).astype(jnp.bfloat16)

    shard = talker_row // row_count
    place = talker_row % row_count
    same = shard[None, :] == shard[:, None]
    earlier = jnp.arange(row_count)[None, :] < jnp.arange(row_count)[:, None]
    order = jnp.sum((same & earlier).astype(jnp.int32), 1)
    step = jnp.arange(step_count, dtype=jnp.int32)[:, None]
    slot = ((shard * step_count + step) * CAP + order).reshape(rows)
    slots = n_dp * step_count * CAP
    pick = slot[None, :] == jnp.arange(slots, dtype=jnp.int32)[:, None]
    spare = -talk_cols % 128
    place_cols = jnp.broadcast_to(
        jnp.tile(narrow(place + 1), step_count)[:, None], (rows, spare)
    )
    sent = jnp.dot(narrow(pick), jnp.concatenate([normed, place_cols], 1))
    got = lax.all_to_all(
        sent.reshape(n_dp, slots // n_dp, -1), "dp", 0, 0, tiled=True
    ).reshape(slots, -1)
    got_place = got[:, talk_cols].astype(jnp.int32) - 1
    got_step = jnp.arange(slots, dtype=jnp.int32) // CAP % step_count
    got_row = jnp.where(got_place < 0, rows, got_step * row_count + got_place)
    put = got_row[None, :] == jnp.arange(rows, dtype=jnp.int32)[:, None]
    talker_input = jnp.dot(narrow(put), got[:, :talk_cols])
    return (
        hidden.reshape(step_count, row_count, -1),
        talker_input.reshape(step_count, row_count, -1),
    )


def solution(mesh):
    placed = (
        P(None, "dp", "mp"),
        P(None, "dp", "mp"),
        P(None, "dp", "mp"),
        P("dp", "mp", None, None),
        P("dp", "mp", None, None),
        P("dp"),
        P("dp"),
        P(None, "dp", "mp"),
        P(None, "dp", "mp"),
        P("mp", None),
        P(None, "mp"),
        P("mp"),
    )
    return jax.shard_map(
        local,
        mesh=mesh,
        in_specs=placed,
        out_specs=(P(None, "dp", "mp"), P(None, "dp", "mp")),
        check_vma=False,
    )
```

```python
import jax
import jax.numpy as jnp
from jax import lax
from jax.experimental import pallas as pl
from jax.experimental.pallas import tpu as pltpu
from jax.sharding import PartitionSpec as P

epsilon = 1e-06
CAP = 10


def attend_and_project(query, token_keys, token_values, cache_keys, stored_values, lengths, out_weight, blocks):
    step_count, row_count, query_cols = query.shape
    head_dim = cache_keys.shape[-1]
    slot_count = cache_keys.shape[-2]
    groups = query_cols // head_dim
    streams = 16
    each = step_count * groups
    fresh = step_count * streams
    padded = max(fresh, slot_count)
    chunks = row_count // streams
    rows = step_count * row_count
    count = blocks.shape[0]
    cols = query_cols
    scale = 1.0 / head_dim**0.5

    def body(blocks_ref, len_ref, q_ref, tk_ref, tv_ref, k_ref, v_ref, w_ref, ctx_ref, *rest):
        out_refs, (w_buf, sems) = rest[:count], rest[count:]
        chunk = pl.program_id(0)

        def load(k):
            at = pl.ds(pl.multiple_of(blocks_ref[k] * cols, cols), cols)
            return pltpu.make_async_copy(w_ref.at[:, at], w_buf.at[k], sems.at[k])

        @pl.when(chunk == 0)
        def _():
            for k in range(count):
                load(k).start()

        q = q_ref[...].reshape(step_count, streams, groups, head_dim)
        q = jnp.swapaxes(q, 0, 1).reshape(streams, each, head_dim)
        scores = (
            lax.dot_general(
                q, k_ref[...], (((2,), (2,)), ((0,), (0,))), preferred_element_type=jnp.float32
            )
            * scale
        )
        slot = lax.broadcasted_iota(jnp.int32, (1, 1, slot_count), 2)
        filled = jnp.concatenate(
            [slot < len_ref[chunk * streams + b] for b in range(streams)]
        )
        scores = jnp.where(filled, scores, -1e30)
        q = q.reshape(streams * each, head_dim)
        copies = padded // fresh
        keys = jnp.concatenate([tk_ref[...].reshape(fresh, head_dim)] * copies)
        values = jnp.concatenate([tv_ref[...].reshape(fresh, head_dim)] * copies)
        recent = (
            lax.dot_general(
                q,
                keys,
                (((1,), (1,)), ((), ())),
                preferred_element_type=jnp.float32,
            )
            * scale
        )
        row = lax.broadcasted_iota(jnp.int32, (streams * each, padded), 0)
        col = lax.broadcasted_iota(jnp.int32, (streams * each, padded), 1)
        mine = (row // each == col % streams) & (col // streams <= row // groups % step_count)
        recent = jnp.where(mine, recent, -1e30).reshape(streams, each, padded)
        highest = jnp.max(jnp.maximum(scores, recent), -1, keepdims=True)
        scores, recent = jnp.exp(scores - highest), jnp.exp(recent - highest)
        scores = scores.astype(jnp.bfloat16)
        recent = recent.astype(jnp.bfloat16).reshape(streams * each, padded)
        context = lax.dot_general(
            scores, v_ref[...], (((2,), (1,)), ((0,), (0,))), preferred_element_type=jnp.float32
        ).reshape(streams * each, head_dim)
        context += jnp.dot(recent, values, preferred_element_type=jnp.float32)
        ones = jnp.ones((padded, head_dim), jnp.bfloat16)
        total = jnp.dot(recent, ones, preferred_element_type=jnp.float32)
        total += jnp.dot(
            scores.reshape(streams * each, slot_count), ones, preferred_element_type=jnp.float32
        )
        context /= total
        context = jnp.swapaxes(context.reshape(streams, step_count, groups, head_dim), 0, 1)
        context = context.reshape(step_count, streams, cols).astype(jnp.bfloat16)
        for t in range(step_count):
            at = pl.ds(pl.multiple_of(t * row_count + chunk * streams, streams), streams)
            ctx_ref[at, :] = context[t]

        @pl.when(chunk == chunks - 1)
        def _():
            for k in range(count):
                load(k).wait()
                out_refs[k][...] = jnp.dot(
                    ctx_ref[...], w_buf[k], preferred_element_type=jnp.float32
                ).astype(jnp.bfloat16)

    def by_stream(*shape):
        return pl.BlockSpec(shape, lambda i, *_: (i,) + (0,) * (len(shape) - 1))

    def by_step(width):
        return pl.BlockSpec((step_count, streams, width), lambda i, *_: (0, i, 0))

    whole = pl.BlockSpec((rows, cols), lambda i, *_: (0, 0))
    return pl.pallas_call(
        body,
        grid_spec=pltpu.PrefetchScalarGridSpec(
            num_scalar_prefetch=2,
            grid=(chunks,),
            in_specs=[
                by_step(query_cols),
                by_step(head_dim),
                by_step(head_dim),
                by_stream(streams, slot_count, head_dim),
                by_stream(streams, slot_count, head_dim),
                pl.BlockSpec(memory_space=pltpu.HBM),
            ],
            out_specs=[whole] * (1 + count),
            scratch_shapes=[
                pltpu.VMEM((count, out_weight.shape[0], cols), jnp.bfloat16),
                pltpu.SemaphoreType.DMA((count,)),
            ],
        ),
        out_shape=[jax.ShapeDtypeStruct((rows, cols), jnp.bfloat16)] * (1 + count),
        compiler_params=pltpu.CompilerParams(vmem_limit_bytes=40 << 20),
        cost_estimate=pl.CostEstimate(
            flops=2 * count * rows * cols * cols,
            bytes_accessed=32 << 20,
            transcendentals=0,
        ),
    )(
        blocks,
        in_hbm(lengths),
        in_hbm(query),
        in_hbm(token_keys),
        in_hbm(token_values),
        in_hbm(cache_keys.reshape(row_count, slot_count, head_dim)),
        in_hbm(stored_values.reshape(row_count, slot_count, head_dim)),
        in_hbm(out_weight),
    )


def head_product(context, out_weight, blocks):
    rows, depth = context.shape
    count = blocks.shape[0]
    cols = out_weight.shape[1] // lax.axis_size("mp")

    def body(blocks_ref, context_ref, w_ref, *rest):
        out_refs, (w_buf, sems) = rest[:count], rest[count:]
        loads = []
        for k in range(count):
            at = pl.ds(pl.multiple_of(blocks_ref[k] * cols, cols), cols)
            loads.append(pltpu.make_async_copy(w_ref.at[:, at], w_buf.at[k], sems.at[k]))
            loads[k].start()
        for k in range(count):
            loads[k].wait()
            out_refs[k][...] = jnp.dot(
                context_ref[...], w_buf[k], preferred_element_type=jnp.float32
            ).astype(jnp.bfloat16)

    return pl.pallas_call(
        body,
        in_specs=[
            pl.BlockSpec(memory_space=pltpu.SMEM),
            pl.BlockSpec(memory_space=pltpu.VMEM),
            pl.BlockSpec(memory_space=pltpu.HBM),
        ],
        out_specs=[pl.BlockSpec(memory_space=pltpu.VMEM)] * count,
        out_shape=[jax.ShapeDtypeStruct((rows, cols), jnp.bfloat16)] * count,
        scratch_shapes=[
            pltpu.VMEM((count, depth, cols), jnp.bfloat16),
            pltpu.SemaphoreType.DMA((count,)),
        ],
        compiler_params=pltpu.CompilerParams(vmem_limit_bytes=28 << 20),
        cost_estimate=pl.CostEstimate(
            flops=2 * count * rows * depth * cols,
            bytes_accessed=2 * count * (depth + rows) * cols,
            transcendentals=0,
        ),
    )(blocks, context, in_hbm(out_weight))


def talker_product(total, pieces, proj_columns, blocks):
    depth = pieces[0][0].shape[1]
    rows = sum(part.shape[0] for part in pieces[0])
    sizes = [len(piece) for piece in pieces]
    count = len(pieces)
    cols = proj_columns.shape[0]
    first = [] if total is None else [total]
    parts = [part for piece in pieces for part in piece]

    def body(blocks_ref, w_ref, *refs):
        part_refs, refs = list(refs[: len(parts)]), refs[len(parts) :]
        out_ref = refs[-1]
        for k in range(count):
            piece = jnp.concatenate([part_refs.pop(0)[...] for _ in range(sizes[k])])
            at = pl.ds(pl.multiple_of(blocks_ref[k] * depth, depth), depth)
            product = lax.dot_general(
                piece,
                w_ref[:, at],
                (((1,), (1,)), ((), ())),
                preferred_element_type=jnp.float32,
            )
            if k > 0:
                out_ref[...] += product
            elif total is None:
                out_ref[...] = product
            else:
                out_ref[...] = refs[0][...] + product

    vmem = pl.BlockSpec(memory_space=pltpu.VMEM)
    return pl.pallas_call(
        body,
        in_specs=[
            pl.BlockSpec(memory_space=pltpu.SMEM),
            vmem,
        ]
        + [vmem] * len(parts + first),
        out_specs=vmem,
        out_shape=jax.ShapeDtypeStruct((rows, cols), jnp.float32),
        compiler_params=pltpu.CompilerParams(vmem_limit_bytes=20 << 20),
        cost_estimate=pl.CostEstimate(
            flops=2 * count * rows * depth * cols,
            bytes_accessed=2 * count * (depth * cols + rows * depth),
            transcendentals=0,
        ),
    )(blocks, proj_columns, *parts, *first)


def shift_y(x, by):
    count = lax.axis_size("mp")
    return lax.ppermute(x, "mp", [(i, (i + 2 * by) % count) for i in range(count)])


def onward(x):
    count = lax.axis_size("mp")
    return lax.ppermute(x, "mp", [(i, (i + 2 - 4 * (i % 2)) % count) for i in range(count)])


def across(x, by):
    count = lax.axis_size("mp")
    moves = [(i, (i + 1 + 2 * by if i % 2 == 0 else i - 1 - 2 * by) % count) for i in range(count)]
    return lax.ppermute(x, "mp", moves)


def swap(x):
    return lax.ppermute(x, "mp", [(i, i ^ 1) for i in range(lax.axis_size("mp"))])


def in_hbm(x):
    return pltpu.with_memory_space_constraint(x, pltpu.HBM)


def wide(x):
    return x.astype(jnp.float32)


def narrow(x):
    return x.astype(jnp.bfloat16)


def local(
    query,
    token_keys,
    token_values,
    cache_keys,
    stored_values,
    lengths,
    talker_row,
    residual,
    embedding,
    out_weight,
    talker_proj,
    talker_gain,
):
    step_count, row_count, query_cols = query.shape
    rows = step_count * row_count
    n_dp = lax.axis_size("dp")
    n_mp = lax.axis_size("mp")
    mp = lax.axis_index("mp")
    y, core = mp // 2, mp % 2
    talk_cols = talker_proj.shape[1]

    ahead = 1 - 2 * core

    def blocks(*wanted):
        ids = [(2 * (y + shift)) % n_mp + core + other * ahead for shift, other in wanted]
        return jnp.stack(ids).astype(jnp.int32)

    context, far_away, far_here = attend_and_project(
        query,
        token_keys,
        token_values,
        cache_keys,
        stored_values,
        lengths,
        out_weight,
        blocks((2, 1), (2, 0)),
    )
    far = narrow(wide(far_here) + wide(swap(far_away)))
    far, context = lax.optimization_barrier((far, context))
    far_on = onward(far)
    other_away, other_here, same_away, same_here, own_away, own_here = head_product(
        context,
        out_weight,
        blocks((-ahead, 0), (ahead, 1), (-ahead, 1), (ahead, 0), (0, 1), (0, 0)),
    )
    other_got, same_got = swap(other_away), swap(same_away)
    other = narrow(wide(other_here) + wide(other_got))
    far_on, own_away = lax.optimization_barrier((far_on, own_away))
    own_got = swap(own_away)
    other_in = across(other, 1)
    same_in = onward(narrow(wide(same_here) + wide(same_got) + wide(far_on)))
    residual = residual.reshape(rows, -1)
    embedding = embedding.reshape(rows, -1)

    base = wide(residual) + wide(own_here) + wide(own_got) + wide(other_in)
    base = lax.optimization_barrier(base)
    hidden = narrow(base + wide(same_in))
    both = hidden + embedding

    proj_columns = talker_proj.T
    near = onward(both)
    cross = across(both, -1)
    both_got = swap(both)
    beyond = onward(near)
    mixed = talker_product(None, [[both_got], [both]], proj_columns, blocks((0, 1), (0, 0)))
    near_got = swap(near)
    mixed = talker_product(
        mixed, [[near_got], [near]], proj_columns, blocks((ahead, 1), (-ahead, 0))
    )
    cross_got = swap(cross)
    mixed = talker_product(
        mixed, [[cross_got], [cross]], proj_columns, blocks((ahead, 0), (-ahead, 1))
    )
    beyond, mixed = lax.optimization_barrier((beyond, mixed))
    mixed = talker_product(mixed, [[beyond]], proj_columns, blocks((2, 0)))
    mixed = talker_product(mixed, [[swap(beyond)]], proj_columns, blocks((2, 1)))

    squares = jnp.sum(mixed * mixed, -1)
    squares = squares + swap(squares)
    beside = onward(squares)
    squares = squares + shift_y(squares, 2) + (beside + swap(beside))
    normed = (
        mixed
        * lax.rsqrt(squares / (talk_cols * n_mp) + epsilon)[:, None]
        * wide(talker_gain)
    ).astype(jnp.bfloat16)

    shard = talker_row // row_count
    place = talker_row % row_count
    same = shard[None, :] == shard[:, None]
    earlier = jnp.arange(row_count)[None, :] < jnp.arange(row_count)[:, None]
    order = jnp.sum((same & earlier).astype(jnp.int32), 1)
    step = jnp.arange(step_count, dtype=jnp.int32)[:, None]
    slot = ((shard * step_count + step) * CAP + order).reshape(rows)
    slots = n_dp * step_count * CAP
    pick = slot[None, :] == jnp.arange(slots, dtype=jnp.int32)[:, None]
    spare = -talk_cols % 128
    place_cols = jnp.broadcast_to(
        jnp.tile(narrow(place + 1), step_count)[:, None], (rows, spare)
    )
    sent = jnp.dot(narrow(pick), jnp.concatenate([normed, place_cols], 1))
    got = lax.all_to_all(
        sent.reshape(n_dp, slots // n_dp, -1), "dp", 0, 0, tiled=True
    ).reshape(slots, -1)
    got_place = got[:, talk_cols].astype(jnp.int32) - 1
    got_step = jnp.arange(slots, dtype=jnp.int32) // CAP % step_count
    got_row = jnp.where(got_place < 0, rows, got_step * row_count + got_place)
    put = got_row[None, :] == jnp.arange(rows, dtype=jnp.int32)[:, None]
    talker_input = jnp.dot(narrow(put), got[:, :talk_cols])
    return (
        hidden.reshape(step_count, row_count, -1),
        talker_input.reshape(step_count, row_count, -1),
    )


def solution(mesh):
    placed = (
        P(None, "dp", "mp"),
        P(None, "dp", "mp"),
        P(None, "dp", "mp"),
        P("dp", "mp", None, None),
        P("dp", "mp", None, None),
        P("dp"),
        P("dp"),
        P(None, "dp", "mp"),
        P(None, "dp", "mp"),
        P("mp", None),
        P(None, "mp"),
        P("mp"),
    )
    return jax.shard_map(
        local,
        mesh=mesh,
        in_specs=placed,
        out_specs=(P(None, "dp", "mp"), P(None, "dp", "mp")),
        check_vma=False,
    )
```

```python
import jax
import jax.numpy as jnp
from jax import lax
from jax.experimental import pallas as pl
from jax.experimental.pallas import tpu as pltpu
from jax.sharding import PartitionSpec as P

epsilon = 1e-06
CAP = 10


def attend_and_project(query, token_keys, token_values, cache_keys, stored_values, lengths, out_weight, blocks):
    step_count, row_count, query_cols = query.shape
    head_dim = cache_keys.shape[-1]
    slot_count = cache_keys.shape[-2]
    groups = query_cols // head_dim
    streams = 16
    each = step_count * groups
    fresh = step_count * streams
    padded = max(fresh, slot_count)
    chunks = row_count // streams
    rows = step_count * row_count
    count = blocks.shape[0]
    cols = query_cols
    scale = 1.0 / head_dim**0.5

    def body(blocks_ref, len_ref, q_ref, tk_ref, tv_ref, k_ref, v_ref, w_ref, ctx_ref, *rest):
        out_refs, (w_buf, sems) = rest[:count], rest[count:]
        chunk = pl.program_id(0)

        def load(k):
            at = pl.ds(pl.multiple_of(blocks_ref[k] * cols, cols), cols)
            return pltpu.make_async_copy(w_ref.at[:, at], w_buf.at[k], sems.at[k])

        @pl.when(chunk == 1)
        def _():
            for k in range(count):
                load(k).start()

        q = q_ref[...].reshape(step_count, streams, groups, head_dim)
        q = jnp.swapaxes(q, 0, 1).reshape(streams, each, head_dim)
        scores = (
            lax.dot_general(
                q, k_ref[...], (((2,), (2,)), ((0,), (0,))), preferred_element_type=jnp.float32
            )
            * scale
        )
        slot = lax.broadcasted_iota(jnp.int32, (1, 1, slot_count), 2)
        filled = jnp.concatenate(
            [slot < len_ref[chunk * streams + b] for b in range(streams)]
        )
        scores = jnp.where(filled, scores, -1e30)
        q = q.reshape(streams * each, head_dim)
        copies = padded // fresh
        keys = jnp.concatenate([tk_ref[...].reshape(fresh, head_dim)] * copies)
        values = jnp.concatenate([tv_ref[...].reshape(fresh, head_dim)] * copies)
        recent = (
            lax.dot_general(
                q,
                keys,
                (((1,), (1,)), ((), ())),
                preferred_element_type=jnp.float32,
            )
            * scale
        )
        row = lax.broadcasted_iota(jnp.int32, (streams * each, padded), 0)
        col = lax.broadcasted_iota(jnp.int32, (streams * each, padded), 1)
        mine = (row // each == col % streams) & (col // streams <= row // groups % step_count)
        recent = jnp.where(mine, recent, -1e30).reshape(streams, each, padded)
        highest = jnp.max(jnp.maximum(scores, recent), -1, keepdims=True)
        scores, recent = jnp.exp(scores - highest), jnp.exp(recent - highest)
        scores = scores.astype(jnp.bfloat16)
        recent = recent.astype(jnp.bfloat16).reshape(streams * each, padded)
        context = lax.dot_general(
            scores, v_ref[...], (((2,), (1,)), ((0,), (0,))), preferred_element_type=jnp.float32
        ).reshape(streams * each, head_dim)
        context += jnp.dot(recent, values, preferred_element_type=jnp.float32)
        ones = jnp.ones((padded, head_dim), jnp.bfloat16)
        total = jnp.dot(recent, ones, preferred_element_type=jnp.float32)
        total += jnp.dot(
            scores.reshape(streams * each, slot_count), ones, preferred_element_type=jnp.float32
        )
        context /= total
        context = jnp.swapaxes(context.reshape(streams, step_count, groups, head_dim), 0, 1)
        context = context.reshape(step_count, streams, cols).astype(jnp.bfloat16)
        for t in range(step_count):
            at = pl.ds(pl.multiple_of(t * row_count + chunk * streams, streams), streams)
            ctx_ref[at, :] = context[t]

        @pl.when(chunk == chunks - 1)
        def _():
            for k in range(count):
                load(k).wait()
                out_refs[k][...] = jnp.dot(
                    ctx_ref[...], w_buf[k], preferred_element_type=jnp.float32
                ).astype(jnp.bfloat16)

    def by_stream(*shape):
        return pl.BlockSpec(shape, lambda i, *_: (i,) + (0,) * (len(shape) - 1))

    def by_step(width):
        return pl.BlockSpec((step_count, streams, width), lambda i, *_: (0, i, 0))

    whole = pl.BlockSpec((rows, cols), lambda i, *_: (0, 0))
    return pl.pallas_call(
        body,
        grid_spec=pltpu.PrefetchScalarGridSpec(
            num_scalar_prefetch=2,
            grid=(chunks,),
            in_specs=[
                by_step(query_cols),
                by_step(head_dim),
                by_step(head_dim),
                by_stream(streams, slot_count, head_dim),
                by_stream(streams, slot_count, head_dim),
                pl.BlockSpec(memory_space=pltpu.HBM),
            ],
            out_specs=[whole] * (1 + count),
            scratch_shapes=[
                pltpu.VMEM((count, out_weight.shape[0], cols), jnp.bfloat16),
                pltpu.SemaphoreType.DMA((count,)),
            ],
        ),
        out_shape=[jax.ShapeDtypeStruct((rows, cols), jnp.bfloat16)] * (1 + count),
        compiler_params=pltpu.CompilerParams(vmem_limit_bytes=40 << 20),
        cost_estimate=pl.CostEstimate(
            flops=2 * count * rows * cols * cols,
            bytes_accessed=32 << 20,
            transcendentals=0,
        ),
    )(
        blocks,
        in_hbm(lengths),
        in_hbm(query),
        in_hbm(token_keys),
        in_hbm(token_values),
        in_hbm(cache_keys.reshape(row_count, slot_count, head_dim)),
        in_hbm(stored_values.reshape(row_count, slot_count, head_dim)),
        in_hbm(out_weight),
    )


def head_product(context, out_weight, blocks):
    rows, depth = context.shape
    count = blocks.shape[0]
    cols = out_weight.shape[1] // lax.axis_size("mp")

    def body(blocks_ref, context_ref, w_ref, *rest):
        out_refs, (w_buf, sems) = rest[:count], rest[count:]
        loads = []
        for k in range(count):
            at = pl.ds(pl.multiple_of(blocks_ref[k] * cols, cols), cols)
            loads.append(pltpu.make_async_copy(w_ref.at[:, at], w_buf.at[k], sems.at[k]))
            loads[k].start()
        for k in range(count):
            loads[k].wait()
            out_refs[k][...] = jnp.dot(
                context_ref[...], w_buf[k], preferred_element_type=jnp.float32
            ).astype(jnp.bfloat16)

    return pl.pallas_call(
        body,
        in_specs=[
            pl.BlockSpec(memory_space=pltpu.SMEM),
            pl.BlockSpec(memory_space=pltpu.VMEM),
            pl.BlockSpec(memory_space=pltpu.HBM),
        ],
        out_specs=[pl.BlockSpec(memory_space=pltpu.VMEM)] * count,
        out_shape=[jax.ShapeDtypeStruct((rows, cols), jnp.bfloat16)] * count,
        scratch_shapes=[
            pltpu.VMEM((count, depth, cols), jnp.bfloat16),
            pltpu.SemaphoreType.DMA((count,)),
        ],
        compiler_params=pltpu.CompilerParams(vmem_limit_bytes=28 << 20),
        cost_estimate=pl.CostEstimate(
            flops=2 * count * rows * depth * cols,
            bytes_accessed=2 * count * (depth + rows) * cols,
            transcendentals=0,
        ),
    )(blocks, context, in_hbm(out_weight))


def talker_product(total, pieces, proj_columns, blocks):
    depth = pieces[0][0].shape[1]
    rows = sum(part.shape[0] for part in pieces[0])
    sizes = [len(piece) for piece in pieces]
    count = len(pieces)
    cols = proj_columns.shape[0]
    first = [] if total is None else [total]
    parts = [part for piece in pieces for part in piece]

    def body(blocks_ref, w_ref, *refs):
        part_refs, refs = list(refs[: len(parts)]), refs[len(parts) :]
        out_ref = refs[-1]
        for k in range(count):
            piece = jnp.concatenate([part_refs.pop(0)[...] for _ in range(sizes[k])])
            at = pl.ds(pl.multiple_of(blocks_ref[k] * depth, depth), depth)
            product = lax.dot_general(
                piece,
                w_ref[:, at],
                (((1,), (1,)), ((), ())),
                preferred_element_type=jnp.float32,
            )
            if k > 0:
                out_ref[...] += product
            elif total is None:
                out_ref[...] = product
            else:
                out_ref[...] = refs[0][...] + product

    vmem = pl.BlockSpec(memory_space=pltpu.VMEM)
    return pl.pallas_call(
        body,
        in_specs=[
            pl.BlockSpec(memory_space=pltpu.SMEM),
            vmem,
        ]
        + [vmem] * len(parts + first),
        out_specs=vmem,
        out_shape=jax.ShapeDtypeStruct((rows, cols), jnp.float32),
        compiler_params=pltpu.CompilerParams(vmem_limit_bytes=20 << 20),
        cost_estimate=pl.CostEstimate(
            flops=2 * count * rows * depth * cols,
            bytes_accessed=2 * count * (depth * cols + rows * depth),
            transcendentals=0,
        ),
    )(blocks, proj_columns, *parts, *first)


def shift_y(x, by):
    count = lax.axis_size("mp")
    return lax.ppermute(x, "mp", [(i, (i + 2 * by) % count) for i in range(count)])


def onward(x):
    count = lax.axis_size("mp")
    return lax.ppermute(x, "mp", [(i, (i + 2 - 4 * (i % 2)) % count) for i in range(count)])


def across(x, by):
    count = lax.axis_size("mp")
    moves = [(i, (i + 1 + 2 * by if i % 2 == 0 else i - 1 - 2 * by) % count) for i in range(count)]
    return lax.ppermute(x, "mp", moves)


def swap(x):
    return lax.ppermute(x, "mp", [(i, i ^ 1) for i in range(lax.axis_size("mp"))])


def in_hbm(x):
    return pltpu.with_memory_space_constraint(x, pltpu.HBM)


def wide(x):
    return x.astype(jnp.float32)


def narrow(x):
    return x.astype(jnp.bfloat16)


def local(
    query,
    token_keys,
    token_values,
    cache_keys,
    stored_values,
    lengths,
    talker_row,
    residual,
    embedding,
    out_weight,
    talker_proj,
    talker_gain,
):
    step_count, row_count, query_cols = query.shape
    rows = step_count * row_count
    n_dp = lax.axis_size("dp")
    n_mp = lax.axis_size("mp")
    mp = lax.axis_index("mp")
    y, core = mp // 2, mp % 2
    talk_cols = talker_proj.shape[1]

    ahead = 1 - 2 * core

    def blocks(*wanted):
        ids = [(2 * (y + shift)) % n_mp + core + other * ahead for shift, other in wanted]
        return jnp.stack(ids).astype(jnp.int32)

    context, far_away, far_here = attend_and_project(
        query,
        token_keys,
        token_values,
        cache_keys,
        stored_values,
        lengths,
        out_weight,
        blocks((2, 1), (2, 0)),
    )
    far = narrow(wide(far_here) + wide(swap(far_away)))
    far, context = lax.optimization_barrier((far, context))
    far_on = onward(far)
    other_away, other_here, same_away, same_here, own_away, own_here = head_product(
        context,
        out_weight,
        blocks((-ahead, 0), (ahead, 1), (-ahead, 1), (ahead, 0), (0, 1), (0, 0)),
    )
    other_got, same_got = swap(other_away), swap(same_away)
    other = narrow(wide(other_here) + wide(other_got))
    far_on, own_away = lax.optimization_barrier((far_on, own_away))
    own_got = swap(own_away)
    other_in = across(other, 1)
    same_in = onward(narrow(wide(same_here) + wide(same_got) + wide(far_on)))
    residual = residual.reshape(rows, -1)
    embedding = embedding.reshape(rows, -1)

    base = wide(residual) + wide(own_here) + wide(own_got) + wide(other_in)
    base = lax.optimization_barrier(base)
    hidden = narrow(base + wide(same_in))
    both = hidden + embedding

    proj_columns = talker_proj.T
    near = onward(both)
    cross = across(both, -1)
    both_got = swap(both)
    beyond = onward(near)
    mixed = talker_product(None, [[both_got], [both]], proj_columns, blocks((0, 1), (0, 0)))
    near_got = swap(near)
    mixed = talker_product(
        mixed, [[near_got], [near]], proj_columns, blocks((ahead, 1), (-ahead, 0))
    )
    cross_got = swap(cross)
    mixed = talker_product(
        mixed, [[cross_got], [cross]], proj_columns, blocks((ahead, 0), (-ahead, 1))
    )
    beyond, mixed = lax.optimization_barrier((beyond, mixed))
    mixed = talker_product(mixed, [[beyond]], proj_columns, blocks((2, 0)))
    mixed = talker_product(mixed, [[swap(beyond)]], proj_columns, blocks((2, 1)))

    squares = jnp.sum(mixed * mixed, -1)
    squares = squares + swap(squares)
    beside = onward(squares)
    squares = squares + shift_y(squares, 2) + (beside + swap(beside))
    normed = (
        mixed
        * lax.rsqrt(squares / (talk_cols * n_mp) + epsilon)[:, None]
        * wide(talker_gain)
    ).astype(jnp.bfloat16)

    shard = talker_row // row_count
    place = talker_row % row_count
    same = shard[None, :] == shard[:, None]
    earlier = jnp.arange(row_count)[None, :] < jnp.arange(row_count)[:, None]
    order = jnp.sum((same & earlier).astype(jnp.int32), 1)
    step = jnp.arange(step_count, dtype=jnp.int32)[:, None]
    slot = ((shard * step_count + step) * CAP + order).reshape(rows)
    slots = n_dp * step_count * CAP
    pick = slot[None, :] == jnp.arange(slots, dtype=jnp.int32)[:, None]
    spare = -talk_cols % 128
    place_cols = jnp.broadcast_to(
        jnp.tile(narrow(place + 1), step_count)[:, None], (rows, spare)
    )
    sent = jnp.dot(narrow(pick), jnp.concatenate([normed, place_cols], 1))
    got = lax.all_to_all(
        sent.reshape(n_dp, slots // n_dp, -1), "dp", 0, 0, tiled=True
    ).reshape(slots, -1)
    got_place = got[:, talk_cols].astype(jnp.int32) - 1
    got_step = jnp.arange(slots, dtype=jnp.int32) // CAP % step_count
    got_row = jnp.where(got_place < 0, rows, got_step * row_count + got_place)
    put = got_row[None, :] == jnp.arange(rows, dtype=jnp.int32)[:, None]
    talker_input = jnp.dot(narrow(put), got[:, :talk_cols])
    return (
        hidden.reshape(step_count, row_count, -1),
        talker_input.reshape(step_count, row_count, -1),
    )


def solution(mesh):
    placed = (
        P(None, "dp", "mp"),
        P(None, "dp", "mp"),
        P(None, "dp", "mp"),
        P("dp", "mp", None, None),
        P("dp", "mp", None, None),
        P("dp"),
        P("dp"),
        P(None, "dp", "mp"),
        P(None, "dp", "mp"),
        P("mp", None),
        P(None, "mp"),
        P("mp"),
    )
    return jax.shard_map(
        local,
        mesh=mesh,
        in_specs=placed,
        out_specs=(P(None, "dp", "mp"), P(None, "dp", "mp")),
        check_vma=False,
    )
```
